256 devices in a mesh: grp: 16 (over x_hi, y, core), tile: 16 (over z, x_lo).
Axes of the slice: x: 4 (x_hi: 2, x_lo: 2; x = x_hi * 2 + x_lo), y: 4, z: 8, core: 2. Of those that a mesh axis runs over, the one named last changes fastest.
Arguments:
- features: float32 [16, 16, 9, 2, 8, 512], P('grp', 'tile'), may hold values from -150 to 150
- lengths: int32 [16], replicated, may hold values from 1 to 9, as said below
- offsets: int32 [16], P('tile'), may hold values from 0 to 15
- norm_gain: float32 [512], replicated, may hold values from 0.1 to 1.9
- norm_bias: float32 [512], replicated, may hold values from -3 to 3
- time_weight: float32 [3, 512, 1024], replicated, may hold values from -0.15625 to 0.15625
- time_bias: float32 [1024], replicated, may hold values from -2 to 2
- space_weight: float32 [3, 3, 512, 256], replicated, may hold values from -0.09375 to 0.09375
- space_bias: float32 [256], replicated, may hold values from -3 to 3
Outputs:
- upsampled_tiles: float32 [16, 16, 18, 4, 16, 256], P('grp', 'tile')
The draws below stay inside these ranges and needn't reach their ends.
Inputs may be any that keep to these rules, and one draw needn't show every extreme that they name: `lengths`: at least one video has all 9 frames.
All inputs are finite; a program needn't handle non-finite values.
Results may differ from the reference program's by a relative error of at most 0.0003.
Values sent between devices are 32-bit elements; how exact they have to be, the bound alone decides.
A program may use at most 128 MiB of HBM per device.

```python
import math
import jax
import jax.numpy as jnp
import numpy as np
from jax import lax

C = 512
C_OUT = 256
GROUPS = 32
FRAMES = 9
LH = 2
LW = 8
VIDEOS = 16
TILES = 16


def draw_features(key, part):
    key = jax.random.fold_in(key, 11)
    key_base, key_pixel, key_chan = jax.random.split(key, 3)
    draw_shape = (VIDEOS, TILES, FRAMES, LH, LW, C)
    base_draw = jnp.clip(jax.random.normal(key_base, draw_shape, jnp.float32), -5.0, 5.0)
    log_top = math.log(10.0)
    pixel_scale = jnp.exp(jax.random.uniform(key_pixel, (VIDEOS, TILES, FRAMES, LH, LW, 1), jnp.float32, 0.0, log_top))
    chan_scale = jnp.exp(jax.random.uniform(key_chan, (C,), jnp.float32, 0.0, math.log(10.0)))
    tile_ramp = 1.0 + 2.0 * jnp.arange(TILES, dtype=jnp.float32) / max(TILES - 1, 1)
    return 0.1 * base_draw * pixel_scale * chan_scale * tile_ramp.reshape(1, TILES, 1, 1, 1, 1)


def draw_lengths(key, part):
    key = jax.random.fold_in(key, 23)
    key_length, key_full = jax.random.split(key)
    drawn_lengths = jax.random.randint(key_length, (VIDEOS,), 1, FRAMES + 1)
    full_video = jax.random.randint(key_full, (), 0, VIDEOS)
    return jnp.where(jnp.arange(VIDEOS) == full_video, FRAMES, drawn_lengths).astype(jnp.int32)


def touch_ends(values, key, least, high):
    spot = [jax.random.randint(jax.random.fold_in(key, axis), (), 0, length) for axis, length in enumerate(values.shape)]
    widest = values.shape.index(max(values.shape))
    neighbour = spot[:widest] + [(spot[widest] + 1) % values.shape[widest]] + spot[widest + 1:]
    return values.at[tuple(spot)].set(least).at[tuple(neighbour)].set(high)


def centred(own_key, dims, spread, limit, kind=jnp.bfloat16):
    entries = spread * jax.random.normal(own_key, dims, jnp.float32)
    return jnp.clip(entries, min=-limit, max=limit).astype(kind)


def setup_inputs(seed: int = 0) -> dict:
    key_of = jax.random.split(jax.random.key(seed), 10)
    return {
        "features": draw_features(jax.random.fold_in(key_of[9], 71), 0),
        "lengths": draw_lengths(jax.random.fold_in(key_of[9], 71), 0),
        "offsets": touch_ends(jax.random.randint(key_of[2], (TILES,), 0, VIDEOS), jax.random.fold_in(key_of[2], 1), 0, VIDEOS - 1).astype(jnp.int32),
        "norm_gain": jnp.clip(1.0 + 0.18 * jax.random.normal(key_of[3], (C,), jnp.float32), 0.1, 1.9),
        "norm_bias": centred(key_of[4], (C,), 0.5, 3.0, jnp.float32),
        "time_weight": centred(key_of[5], (3, C, 2 * C), (3 * C) ** -0.5, 0.15625, jnp.float32),
        "time_bias": centred(key_of[6], (2 * C,), 0.3, 2.0, jnp.float32),
        "space_weight": centred(key_of[7], (3, 3, C, C_OUT), (9 * C) ** -0.5, 0.09375, jnp.float32),
        "space_bias": centred(key_of[8], (C_OUT,), 0.5, 3.0, jnp.float32),
    }


tap_select = np.array([[[1, 0, 0], [0, 1, 1]], [[1, 1, 0], [0, 0, 1]]], dtype=np.float32)

def phase_weights(space_weight):
    select = jnp.asarray(tap_select).astype(space_weight.dtype)
    return jnp.einsum('apk,bql,klio->abpqio', select, select, space_weight, precision=lax.Precision.HIGHEST)

def decode_block(padded, length, border, time_weight, time_bias, phases, space_bias):
    frames, height_pad, width_pad, channels = padded.shape
    height = height_pad - 2
    width_in = width_pad - 2
    leading = jnp.zeros((2, height_pad, width_pad, channels), padded.dtype)
    history = jnp.concatenate([leading, padded], axis=0)
    temporal = jnp.zeros((frames * height_pad * width_pad, 2 * channels), padded.dtype) + time_bias
    for tap_index in range(3):
        window = history[tap_index:tap_index + frames].reshape(-1, channels)
        temporal = temporal + jnp.dot(window, time_weight[tap_index], precision=lax.Precision.HIGHEST, preferred_element_type=jnp.float32)
    temporal = temporal.reshape(frames, height_pad, width_pad, 2, channels)
    doubled = jnp.moveaxis(temporal, 3, 1).reshape(2 * frames, height_pad, width_pad, channels)
    doubled = doubled * border[None, :, :, None]
    outputs = []
    for phase_row in range(2):
        row_list = []
        for phase_col in range(2):
            total = jnp.zeros((2 * frames * height * width_in, phases.shape[-1]), padded.dtype)
            for tap_row in range(2):
                for tap_col in range(2):
                    top_row = phase_row + tap_row
                    left_col = phase_col + tap_col
                    window = doubled[:, top_row:top_row + height, left_col:left_col + width_in].reshape(-1, channels)
                    total = total + jnp.dot(window, phases[phase_row, phase_col, tap_row, tap_col], precision=lax.Precision.HIGHEST, preferred_element_type=jnp.float32)
            row_list.append(total.reshape(2 * frames, height, width_in, -1))
        outputs.append(jnp.stack(row_list))
    blocks = jnp.stack(outputs)
    outward = jnp.transpose(blocks, (2, 3, 0, 4, 1, 5)).reshape(2 * frames, 2 * height, 2 * width_in, -1) + space_bias
    frame_keep = (jnp.arange(2 * frames) < 2 * length).astype(padded.dtype)
    return outward * frame_keep[:, None, None, None]

def reference(features, lengths, offsets, norm_gain, norm_bias, time_weight, time_bias, space_weight, space_bias):
    tile_cols = TILES // 2
    group_width = C // GROUPS
    phases = phase_weights(space_weight)

    def one_video(operands):
        tiles, length = operands
        frame = tiles.reshape(2, tile_cols, FRAMES, LH, LW, C).transpose(2, 0, 3, 1, 4, 5).reshape(FRAMES, 2 * LH, tile_cols * LW, C)
        frame_keep = (jnp.arange(FRAMES) < length).astype(frame.dtype)
        masked = frame * frame_keep[:, None, None, None]
        sum_first = lax.optimization_barrier(jnp.sum(masked, axis=(0, 1, 2))).reshape(GROUPS, group_width).sum(axis=1)
        sum_second = lax.optimization_barrier(jnp.sum(masked * frame, axis=(0, 1, 2))).reshape(GROUPS, group_width).sum(axis=1)
        total_count = length.astype(frame.dtype) * float(TILES * LH * LW * group_width)
        group_mean = sum_first / total_count
        group_scale = lax.rsqrt(sum_second / total_count - group_mean * group_mean + 1e-06)
        mean_chan = jnp.repeat(group_mean, group_width)
        scale_chan = jnp.repeat(group_scale, group_width)
        active = jax.nn.silu((frame - mean_chan) * scale_chan * norm_gain + norm_bias)
        padded = jnp.pad(active, ((0, 0), (1, 1), (1, 1), (0, 0)))
        border = jnp.pad(jnp.ones((2 * LH, tile_cols * LW), frame.dtype), 1)
        decoded = decode_block(padded, length, border, time_weight, time_bias, phases, space_bias)
        decoded = decoded.reshape(2 * FRAMES, 2, 2 * LH, tile_cols, 2 * LW, C_OUT).transpose(1, 3, 0, 2, 4, 5)
        return decoded.reshape(TILES, 2 * FRAMES, 2 * LH, 2 * LW, C_OUT)
    decoded_all = lax.map(one_video, (features, lengths))
    source = jnp.bitwise_xor(jnp.arange(VIDEOS, dtype=jnp.int32)[:, None], offsets.astype(jnp.int32)[None, :])
    return decoded_all[source, jnp.arange(TILES, dtype=jnp.int32)[None, :]]
```

```python
import jax
import jax.numpy as jnp
from jax import lax
from jax.experimental import pallas as pl
from jax.experimental.pallas import tpu as pltpu
from jax.sharding import PartitionSpec as P

F32, BF16 = jnp.float32, jnp.bfloat16
GROUPS = 32


def split(value):
    high = value.astype(BF16)
    return high, (value - high.astype(F32)).astype(BF16)


def prepare_time(raw, high, low):
    rows = 64
    taps, depth, width = raw.shape

    @pl.loop(0, taps * depth // rows)
    def _(step):
        tap = step // (depth // rows)
        at = pl.ds(pl.multiple_of(step % (depth // rows) * rows, rows), rows)
        high[tap, at], low[tap, at] = split(raw[tap, at])


def prepare_space(raw, high, low):
    rows = 32
    depth = raw.shape[2]

    @pl.loop(0, depth // rows)
    def _(step):
        at = pl.ds(pl.multiple_of(step * rows, rows), rows)
        kernel = [[raw[a, b, at] for b in range(3)] for a in range(3)]
        by_row = [kernel[0], [kernel[0][b] + kernel[1][b] + kernel[2][b] for b in range(3)], kernel[2]]
        for a in range(3):
            one = by_row[a]
            for b, value in enumerate((one[0], one[0] + one[1] + one[2], one[2])):
                high[a * 3 + b, at], low[a * 3 + b, at] = split(value)


def dots(pairs):
    total = None
    for left, right in pairs:
        part = jnp.dot(left, right, preferred_element_type=F32)
        total = part if total is None else total + part
    return total


def normalize(frames, first, block, mean, scale, gain, bias, act_high, act_low):
    for step in range(frames):
        value = block[first + step]
        inner = (value - mean) * scale * gain + bias
        inner = inner / (1.0 + jnp.exp(-inner))
        act_high[first + step + 2], act_low[first + step + 2] = split(inner)


def decode(frames, first, keep, upper, has_left, has_right, act, time, time_bias, space, space_bias, temporal, ops, out):
    (act_high, act_low), (time_high, time_low), (space_high, space_low), (op_high, op_low) = act, time, space, ops
    rows = frames * 32
    depth = act_high.shape[-1]
    pairs = []
    for tap in range(3):
        high = act_high[pl.ds(first + tap, frames)].reshape(rows, depth)
        low = act_low[pl.ds(first + tap, frames)].reshape(rows, depth)
        pairs += [(high, time_high[tap]), (low, time_high[tap]), (high, time_low[tap])]
    temporal[...] = dots(pairs) + time_bias[...]
    place = lax.broadcasted_iota(jnp.int32, (8, depth), 0)
    for frame in range(frames):
        for half in range(2):
            lanes = slice(half * depth, half * depth + depth)
            block = lambda i: temporal[frame * 32 + i * 8:frame * 32 + i * 8 + 8, lanes]
            row0, row1, across, side = block(0), block(1), block(2), block(3)
            columns = []
            for row, left, right in ((row0, 0, 2), (row1, 1, 3), (across, 4, 5)):
                before = jnp.where(place == 0, side[left:left + 1] * has_left, pltpu.roll(row, 1, 0))
                after = jnp.where(place == 7, side[right:right + 1] * has_right, pltpu.roll(row, 7, 0))
                columns.append((before - row, row, after - row))
            start = (frame * 2 + half) * 16
            for b in range(3):
                row0, row1, across = columns[0][b], columns[1][b], columns[2][b]
                above = across * (1.0 - upper)
                below = across * upper
                for a, value in enumerate((
                    jnp.concatenate([above - row0, row0 - row1], axis=0),
                    jnp.concatenate([row0, row1], axis=0),
                    jnp.concatenate([row1 - row0, below - row1], axis=0),
                )):
                    op_high[a * 3 + b, start:start + 16], op_low[a * 3 + b, start:start + 16] = split(value)
    parts = []
    for k in range(9):
        high, low = op_high[k], op_low[k]
        parts.append(dots([(high, space_high[k]), (low, space_high[k]), (high, space_low[k])]))
    for up in range(2):
        base = parts[3 * (2 * up)], parts[3 * (2 * up) + 1], parts[3 * (2 * up) + 2]
        base = [base[b] + parts[3 + b] for b in range(3)]
        for side in range(2):
            value = base[1] + base[2 * side] + space_bias[...]
            for frame in range(frames):
                for half in range(2):
                    start = (frame * 2 + half) * 16
                    valid = (first + frame) < keep
                    for row in range(2):
                        piece = value[start + row * 8:start + row * 8 + 8]
                        piece = jnp.where(valid, piece, 0.0)
                        for lane in range(2):
                            out[lane, (first + frame) * 2 + half, row * 2 + up, pl.ds(side, 8, stride=2), :] = piece[:, lane * 128:lane * 128 + 128]


MESH = pl.DeviceIdType.MESH
ACROSS, RIGHT, LEFT, ACROSS_RIGHT, ACROSS_LEFT = range(5)
MIRROR = (ACROSS, LEFT, RIGHT, ACROSS_LEFT, ACROSS_RIGHT)
SIDES = (RIGHT, RIGHT, LEFT, LEFT, ACROSS_RIGHT, ACROSS_LEFT)
PIECES = ((0, 8, 16), (8, 2, 24), (10, 2, 26), (12, 1, 28), (13, 1, 29))
SENT = 32


def wide(value, times=4):
    return jnp.concatenate([value] * times, axis=-1)


def group_sums(value):
    lane = lax.broadcasted_iota(jnp.int32, value.shape, 1)
    for step in (1, 2, 4, 8):
        ahead, behind = pltpu.roll(value, 128 - step, 1), pltpu.roll(value, step, 1)
        value = value + jnp.where(lane & step == 0, ahead, behind)
    return value


def tile_neighbours(tile):
    column, row = tile % 8, tile // 8
    right, left = (column + 1) % 8, (column + 7) % 8
    own, other = row * 8, (1 - row) * 8
    return other + column, own + right, own + left, other + right, other + left


def gather_kernel(
    offsets, lengths, features, block, stats,
    near, swap_out, swap_in, core_out, core_in, halo, marks, mark_in, kinds, sums, sums_in, norms, norms_in,
    near_sem, swap_sem, core_sem, halo_sem, mark_sem, sums_sem, norms_sem,
):
    frames = features.shape[0]
    grp, tile = lax.axis_index("grp"), lax.axis_index("tile")
    neighbours = tile_neighbours(tile)
    facing = 1 - tile // 8

    def send(source, target, sems, at, device):
        out_sem, in_sem = sems
        return pltpu.make_async_remote_copy(
            src_ref=source, dst_ref=target, send_sem=out_sem.at[at], recv_sem=in_sem.at[at],
            device_id=device, device_id_type=MESH,
        )

    def near_copy(step, frame):
        return send(features.at[frame], near.at[step - 1, frame], near_sem, (step - 1, frame), (grp ^ (step * 2), tile))

    def swap_copy(frame):
        rows = pl.ds(0, SENT)
        return send(swap_out.at[frame, rows], swap_in.at[frame, rows], swap_sem, frame, (grp ^ 8, tile))

    def core_copy(frame):
        rows = pl.ds(0, SENT)
        return send(core_out.at[frame, rows], core_in.at[frame, rows], core_sem, frame, (grp ^ 1, tile))

    def halo_copy(kind, frame):
        start, count, land = PIECES[kind]
        return send(
            halo.at[frame, pl.ds(start, count)], block.at[frame, pl.ds(land, count)],
            halo_sem, (kind, frame), (grp, neighbours[kind]),
        )

    def mark_copy(kind):
        return send(marks, mark_in.at[MIRROR[kind]], mark_sem, MIRROR[kind], (grp, neighbours[kind]))

    def sums_copy(step):
        return send(sums, sums_in.at[step], sums_sem, step, (grp, (tile + step) % 16))

    def norms_copy(step):
        return send(norms, norms_in.at[step], norms_sem, step, (grp ^ step, tile))

    block[:, 24:32] = jnp.zeros((frames, 8, 512), F32)
    barrier = pltpu.get_barrier_semaphore()

    @pl.loop(1, 16)
    def _(step):
        pl.semaphore_signal(barrier, inc=1, device_id=(grp, (tile + step) % 16), device_id_type=MESH)
        pl.semaphore_signal(barrier, inc=1, device_id=(grp ^ step, tile), device_id_type=MESH)

    marks[...] = jnp.full(marks.shape, offsets[0], jnp.int32)
    length = lengths[grp]
    total, squares = jnp.zeros((8, 512), F32), jnp.zeros((8, 512), F32)
    for frame in range(frames):
        for row in range(2):
            value = jnp.where(frame < length, features[frame, row * 8 : row * 8 + 8], 0.0)
            total, squares = total + value, squares + value * value
    total, squares = jnp.sum(total, axis=0, keepdims=True), jnp.sum(squares, axis=0, keepdims=True)
    for part in range(4):
        sums[part : part + 1] = total[:, part * 128 : part * 128 + 128]
        sums[part + 4 : part + 5] = squares[:, part * 128 : part * 128 + 128]

    pl.semaphore_wait(barrier, 30)
    for kind in range(5):
        mark_copy(kind).start()

    @pl.loop(1, 16)
    def _(step):
        sums_copy(step).start()

    @pl.loop(0, frames)
    def _(frame):
        for step in (1, 2, 3):
            near_copy(step, frame).start()

    swap_out[:, 24:32] = jnp.zeros((frames, 8, 512), F32)

    for kind in range(5):
        mark_copy(kind).wait_recv()
    kinds[0] = marks[...]
    kinds[1] = mark_in[ACROSS]
    kinds[2] = jnp.concatenate([mark_in[kind][0:1] for kind in SIDES] + [marks[0:2]], axis=0)

    def chosen(rows, frame, mark):
        pick = wide(mark // 2 % 4)
        value = features[frame, rows]
        for step in (1, 2, 3):
            value = jnp.where(pick == step, near[step - 1, frame, rows], value)
        return value

    def start_swap(frame):
        for step in (1, 2, 3):
            near_copy(step, frame).wait_recv()
        for row in range(2):
            swap_out[frame, row * 8 : row * 8 + 8] = chosen(pl.ds(row * 8, 8), frame, kinds[0])
        swap_out[frame, 16:24] = chosen(pl.ds(pl.multiple_of(facing * 8, 8), 8), frame, kinds[1])
        for place, source in enumerate((7, 15, 0, 8, facing * 8 + 7, facing * 8)):
            mark = kinds[2, place : place + 1]
            swap_out[frame, 24 + place : 25 + place] = chosen(pl.ds(source, 1), frame, mark)
        swap_copy(frame).start()

    def start_core(frame):
        swap_copy(frame).wait_recv()
        for part, kind in enumerate((0, 0, 1, 2)):
            rows = slice(part * 8, part * 8 + 8)
            crossed = wide(kinds[kind]) // 8 == 1
            core_out[frame, rows] = jnp.where(crossed, swap_in[frame, rows], swap_out[frame, rows])
        core_copy(frame).start()

    def start_halo(frame):
        core_copy(frame).wait_recv()
        for part, kind in enumerate((0, 0, 1, 2)):
            rows = slice(part * 8, part * 8 + 8)
            crossed = wide(kinds[kind]) % 2 == 1
            value = jnp.where(crossed, core_in[frame, rows], core_out[frame, rows])
            if part < 2:
                block[frame, rows] = value
            else:
                halo[frame, part * 8 - 16 : part * 8 - 8] = value
        for kind in range(5):
            halo_copy(kind, frame).start()

    @pl.loop(0, frames + 3)
    def _(step):
        @pl.when(step < frames)
        def _():
            start_swap(step)

        @pl.when((step >= 1) & (step < frames + 1))
        def _():
            start_core(step - 1)

        @pl.when((step >= 2) & (step < frames + 2))
        def _():
            start_halo(step - 2)

        @pl.when(step == 1)
        def _():
            @pl.loop(1, 16)
            def _(other):
                sums_copy(other).wait_recv()

            value = sums[...]
            for other in range(1, 16):
                value = value + sums_in[other]
            value = group_sums(value) / (length.astype(F32) * 4096.0)
            mean = value[0:4]
            norms[0:4] = mean
            norms[4:8] = 1.0 / jnp.sqrt(value[4:8] - mean * mean + 1e-6)

            @pl.loop(1, 16)
            def _(other):
                norms_copy(other).start()

        @pl.when(step >= 3)
        def _():
            for kind in range(5):
                halo_copy(kind, step - 3).wait_recv()

    @pl.loop(1, 16)
    def _(other):
        norms_copy(other).wait_recv()

    value = norms[...]
    for other in range(1, 16):
        value = jnp.where(marks[...] == other, norms_in[other], value)
    stats[...] = value

    for kind in range(5):
        mark_copy(kind).wait_send()

    @pl.loop(1, 16)
    def _(other):
        sums_copy(other).wait_send()
        norms_copy(other).wait_send()

    @pl.loop(0, frames)
    def _(frame):
        for step in (1, 2, 3):
            near_copy(step, frame).wait_send()
        swap_copy(frame).wait_send()
        core_copy(frame).wait_send()
        for kind in range(5):
            halo_copy(kind, frame).wait_send()


def gathered(offsets, lengths, features):
    frames = features.shape[0]
    whole, scalars = pl.BlockSpec(memory_space=pltpu.VMEM), pl.BlockSpec(memory_space=pltpu.SMEM)
    sems = lambda *shape: [[pltpu.SemaphoreType.DMA(shape)] * 2]
    buffer = lambda *shape: pltpu.VMEM(shape, F32)
    return pl.pallas_call(
        gather_kernel,
        out_shape=(jax.ShapeDtypeStruct((frames, 32, 512), F32), jax.ShapeDtypeStruct((8, 128), F32)),
        in_specs=[scalars, scalars, whole],
        out_specs=(whole, whole),
        scratch_shapes=[buffer(3, frames, 16, 512)]
        + [buffer(frames, 32, 512)] * 4
        + [buffer(frames, 16, 512)]
        + [pltpu.VMEM(shape, jnp.int32) for shape in ((8, 128), (5, 8, 128), (3, 8, 128))]
        + [buffer(8, 128), buffer(16, 8, 128)] * 2
        + sems(3, frames) + sems(frames) * 2 + sems(5, frames) + sems(5) + sems(16) * 2,
        compiler_params=pltpu.CompilerParams(
            collective_id=0, has_side_effects=True, vmem_limit_bytes=40 * 2**20
        ),
    )(offsets, lengths, features)


def decode_kernel(keep, block, stats, gain, bias, time_raw, time_bias, space_raw, space_bias, result,
                  time_f32, space_f32, time_high, time_low, space_high, space_low, act_high, act_low,
                  temporal, op_high, op_low, out, sem):
    frames = block.shape[0]
    tile = lax.axis_index("tile")
    copies = [pltpu.make_async_copy(time_raw, time_f32, sem.at[0]), pltpu.make_async_copy(space_raw, space_f32, sem.at[1])]
    for copy in copies:
        copy.start()
    act_high[0:2] = jnp.zeros((2, 32, 512), BF16)
    act_low[0:2] = jnp.zeros((2, 32, 512), BF16)
    lanes = lambda row: jnp.concatenate([stats[row + i : row + i + 1] for i in range(4)], axis=1)
    mean, scale = lanes(0), lanes(4)
    normalize(frames, 0, block, mean, scale, gain[...], bias[...], act_high, act_low)
    copies[0].wait()
    prepare_time(time_f32, time_high, time_low)
    copies[1].wait()
    prepare_space(space_f32, space_high, space_low)
    number = lambda flag: flag.astype(F32)
    decode(
        frames, 0, keep[0], number(tile < 8), number(tile % 8 != 0), number(tile % 8 != 7),
        (act_high, act_low), (time_high, time_low), time_bias, (space_high, space_low), space_bias,
        temporal, (op_high, op_low), out,
    )
    copies = [
        pltpu.make_async_copy(out.at[lane], result.at[:, :, :, pl.ds(lane * 128, 128)], sem.at[lane]) for lane in range(2)
    ]
    for copy in copies:
        copy.start()
    for copy in copies:
        copy.wait()


def decoded(keep, block, stats, gain, bias, time_weight, time_bias, space_weight, space_bias):
    frames = block.shape[0]
    whole, scalars, anywhere = (pl.BlockSpec(memory_space=kind) for kind in (pltpu.VMEM, pltpu.SMEM, pl.ANY))
    buffer = lambda kind, *shape: pltpu.VMEM(shape, kind)
    return pl.pallas_call(
        decode_kernel,
        out_shape=jax.ShapeDtypeStruct((2 * frames, 4, 16, 256), F32),
        in_specs=[scalars, whole, whole, whole, whole, anywhere, whole, anywhere, whole],
        out_specs=anywhere,
        scratch_shapes=[buffer(F32, 3, 512, 1024), buffer(F32, 3, 3, 512, 256)]
        + [buffer(BF16, 3, 512, 1024)] * 2
        + [buffer(BF16, 9, 512, 256)] * 2
        + [buffer(BF16, frames + 2, 32, 512)] * 2
        + [buffer(F32, frames * 32, 1024)]
        + [buffer(BF16, 9, frames * 32, 512)] * 2
        + [buffer(F32, 2, 2 * frames, 4, 16, 128), pltpu.SemaphoreType.DMA((2,))],
        compiler_params=pltpu.CompilerParams(vmem_limit_bytes=52 * 2**20),
    )(keep, block, stats, gain, bias, time_weight, time_bias, space_weight, space_bias)


def on_device(features, lengths, offsets, norm_gain, norm_bias, time_weight, time_bias, space_weight, space_bias):
    frames, channels = features.shape[2], features.shape[-1]
    source = lax.axis_index("grp") ^ offsets[0]
    block, stats = gathered(offsets, lengths, features.reshape(frames, 16, channels))
    row = lambda array: array.reshape(1, -1)
    result = decoded(
        lengths[source][None], block, stats, row(norm_gain), row(norm_bias),
        time_weight, row(time_bias), space_weight, row(space_bias),
    )
    return result[None, None]


def solution(mesh):
    in_specs = (P("grp", "tile", None, None, None, None), P(), P("tile"), P(), P(), P(), P(), P(), P())
    out_specs = P("grp", "tile", None, None, None, None)
    return jax.shard_map(on_device, mesh=mesh, in_specs=in_specs, out_specs=out_specs, check_vma=False)
```

```python
import jax
import jax.numpy as jnp
from jax import lax
from jax.experimental import pallas as pl
from jax.experimental.pallas import tpu as pltpu
from jax.sharding import PartitionSpec as P

F32, BF16 = jnp.float32, jnp.bfloat16


def split(value):
    high = value.astype(BF16)
    return high, (value - high.astype(F32)).astype(BF16)


def prepare_time(step, raw, both):
    rows = 64
    depth = raw.shape[1]
    tap = step // (depth // rows)
    at = pl.ds(pl.multiple_of(step % (depth // rows) * rows, rows), rows)
    both[0, tap, at], both[1, tap, at] = split(raw[tap, at])


def prepare_space(step, raw, both):
    rows = 32
    at = pl.ds(pl.multiple_of(step * rows, rows), rows)
    kernel = [[raw[a, b, at] for b in range(3)] for a in range(3)]
    by_row = [kernel[0], [kernel[0][b] + kernel[1][b] + kernel[2][b] for b in range(3)], kernel[2]]
    for a in range(3):
        one = by_row[a]
        for b, value in enumerate((one[0], one[0] + one[1] + one[2], one[2])):
            both[0, a * 3 + b, at], both[1, a * 3 + b, at] = split(value)


def normalize(first, count, block, mean, scale, gain, bias, act):
    for frame in range(first, first + count):
        inner = (block[frame] - mean) * scale * gain + bias
        inner = inner / (1.0 + jnp.exp(-inner))
        act[0, frame + 2], act[1, frame + 2] = split(inner)


def decode(first, frames, keep, upper, has_left, has_right, act, time, time_bias, space, space_bias, temporal, ops, stage, out):
    rows, depth = frames * 32, act.shape[-1]
    both, high = [], []
    for tap in range(3):
        at = pl.ds(first + tap, frames)
        both.append(act[:, at].reshape(2 * rows, depth))
        high.append(act[0, at].reshape(rows, depth))
    weights = time.reshape(2, 3 * depth, 2 * depth)
    product = jnp.dot(jnp.concatenate(both, axis=1), weights[0], preferred_element_type=F32)
    yield
    rest = jnp.dot(jnp.concatenate(high, axis=1), weights[1], preferred_element_type=F32)
    temporal[0:rows] = product[:rows] + product[rows:] + rest + time_bias[...]
    yield
    place = lax.broadcasted_iota(jnp.int32, (8, depth), 0)
    for frame in range(frames):
        for half in range(2):
            lanes = slice(half * depth, half * depth + depth)
            block = lambda i: temporal[frame * 32 + i * 8 : frame * 32 + i * 8 + 8, lanes]
            row0, row1, across, side = block(0), block(1), block(2), block(3)
            columns = []
            for row, left, right in ((row0, 0, 2), (row1, 1, 3), (across, 4, 5)):
                before = jnp.where(place == 0, side[left : left + 1] * has_left, pltpu.roll(row, 1, 0))
                after = jnp.where(place == 7, side[right : right + 1] * has_right, pltpu.roll(row, 7, 0))
                columns.append((before - row, row, after - row))
            start = (frame * 2 + half) * 16
            for b in range(3):
                row0, row1, across = columns[0][b], columns[1][b], columns[2][b]
                above, below = across * (1.0 - upper), across * upper
                for a, value in enumerate((
                    jnp.concatenate([above - row0, row0 - row1], axis=0),
                    jnp.concatenate([row0, row1], axis=0),
                    jnp.concatenate([row1 - row0, below - row1], axis=0),
                )):
                    at = pl.ds(start, 16)
                    ops[a * 3 + b, 0, at], ops[a * 3 + b, 1, at] = split(value)
        yield
    parts = []
    for k in range(9):
        product = jnp.dot(ops[k, :, 0:rows].reshape(2 * rows, depth), space[0, k], preferred_element_type=F32)
        product = product[:rows] + product[rows:]
        parts.append(product + jnp.dot(ops[k, 0, 0:rows], space[1, k], preferred_element_type=F32))
        if k % 3 == 2:
            yield
    for up in range(2):
        base = [parts[6 * up + b] + parts[3 + b] for b in range(3)]
        for side in range(2):
            value = base[1] + base[2 * side] + space_bias[...]
            for frame in range(frames):
                for half in range(2):
                    start = (frame * 2 + half) * 16
                    for row in range(2):
                        piece = value[start + row * 8 : start + row * 8 + 8]
                        for lane in range(2):
                            stage[lane, frame * 2 + half, row * 2 + up, pl.ds(side, 8, stride=2), :] = piece[:, lane * 128 : lane * 128 + 128]
    yield
    for frame in range(frames):
        valid = (first + frame) < keep
        for half in range(2):
            for row in range(4):
                piece = jnp.concatenate([stage[lane, frame * 2 + half, row] for lane in range(2)], axis=1)
                out[(first + frame) * 2 + half, row] = jnp.where(valid, piece, 0.0)
    yield


MESH = pl.DeviceIdType.MESH
ACROSS, RIGHT, LEFT, ACROSS_RIGHT, ACROSS_LEFT = range(5)
MIRROR = (ACROSS, LEFT, RIGHT, ACROSS_LEFT, ACROSS_RIGHT)
SIDES = (RIGHT, RIGHT, LEFT, LEFT, ACROSS_RIGHT, ACROSS_LEFT)
PIECES = ((0, 8, 16), (8, 2, 24), (10, 2, 26), (12, 1, 28), (13, 1, 29))
SENT = 32


def wide(value, times=4):
    return jnp.concatenate([value] * times, axis=-1)


def group_sums(value):
    lane = lax.broadcasted_iota(jnp.int32, value.shape, 1)
    for step in (1, 2, 4, 8):
        ahead, behind = pltpu.roll(value, 128 - step, 1), pltpu.roll(value, step, 1)
        value = value + jnp.where(lane & step == 0, ahead, behind)
    return value


def tile_neighbours(tile):
    column, row = tile % 8, tile // 8
    right, left = (column + 1) % 8, (column + 7) % 8
    own, other = row * 8, (1 - row) * 8
    return other + column, own + right, own + left, other + right, other + left


CORE_AFTER, HALO_AFTER = 2, 3
CHUNKS = (3, 3, 3)
LOOPED = 8


def kernel(
    offsets, lengths, raw_features, gain_in, bias_in, time_in, time_bias_in, space_in, space_bias_in, result,
    features, gain, bias, time_raw, time_bias, space_raw, space_bias,
    near, swap_out, swap_in, core_out, core_in, halo, block,
    marks, mark_in, kinds, sums, sums_in, norms, norms_in,
    time, space, act, temporal, ops, stage, out,
    near_sem, swap_sem, core_sem, halo_sem, mark_sem, sums_sem, norms_sem, load_sem, store_sem,
):
    frames = features.shape[0]
    grp, tile = lax.axis_index("grp"), lax.axis_index("tile")
    neighbours = tile_neighbours(tile)
    facing = 1 - tile // 8

    loads = [
        pltpu.make_async_copy(source, target, load_sem.at[at])
        for at, (source, target) in enumerate((
            (raw_features, features), (time_in, time_raw), (space_in, space_raw), (gain_in, gain),
            (bias_in, bias), (time_bias_in, time_bias), (space_bias_in, space_bias),
        ))
    ]
    for load in loads:
        load.start()

    def send(source, target, sems, at, device):
        out_sem, in_sem = sems
        return pltpu.make_async_remote_copy(
            src_ref=source, dst_ref=target, send_sem=out_sem.at[at], recv_sem=in_sem.at[at],
            device_id=device, device_id_type=MESH,
        )

    def near_copy(step, frame):
        return send(raw_features.at[frame], near.at[step - 1, frame], near_sem, (step - 1, frame), (grp ^ (step * 2), tile))

    def swap_copy(frame):
        rows = pl.ds(0, SENT)
        return send(swap_out.at[frame, rows], swap_in.at[frame, rows], swap_sem, frame, (grp ^ 8, tile))

    def core_copy(frame):
        rows = pl.ds(0, SENT)
        return send(core_out.at[frame, rows], core_in.at[frame, rows], core_sem, frame, (grp ^ 1, tile))

    def halo_copy(kind, frame):
        start, count, land = PIECES[kind]
        return send(
            halo.at[frame, pl.ds(start, count)], block.at[frame, pl.ds(land, count)],
            halo_sem, (kind, frame), (grp, neighbours[kind]),
        )

    def mark_copy(kind):
        return send(marks, mark_in.at[MIRROR[kind]], mark_sem, MIRROR[kind], (grp, neighbours[kind]))

    def sums_copy(step):
        return send(sums, sums_in.at[step], sums_sem, step, (grp, (tile + step) % 16))

    def norms_copy(step):
        return send(norms, norms_in.at[step], norms_sem, step, (grp ^ step, tile))

    block[:, 24:32] = jnp.zeros((frames, 8, 512), F32)
    barrier = pltpu.get_barrier_semaphore()

    @pl.loop(1, 16)
    def _(step):
        pl.semaphore_signal(barrier, inc=1, device_id=(grp, (tile + step) % 16), device_id_type=MESH)
        pl.semaphore_signal(barrier, inc=1, device_id=(grp ^ step, tile), device_id_type=MESH)

    marks[...] = jnp.full(marks.shape, offsets[0], jnp.int32)
    swap_out[:, 24:32] = jnp.zeros((frames, 8, 512), F32)
    act[:, 0:2] = jnp.zeros((2, 2, 32, 512), BF16)
    length = lengths[grp]
    loads[0].wait()
    total, squares = jnp.zeros((8, 512), F32), jnp.zeros((8, 512), F32)
    for frame in range(frames):
        for row in range(2):
            value = jnp.where(frame < length, features[frame, row * 8 : row * 8 + 8], 0.0)
            total, squares = total + value, squares + value * value
    total, squares = jnp.sum(total, axis=0, keepdims=True), jnp.sum(squares, axis=0, keepdims=True)
    for part in range(4):
        sums[part : part + 1] = total[:, part * 128 : part * 128 + 128]
        sums[part + 4 : part + 5] = squares[:, part * 128 : part * 128 + 128]

    pl.semaphore_wait(barrier, 30)
    for kind in range(5):
        mark_copy(kind).start()

    @pl.loop(1, 16)
    def _(step):
        sums_copy(step).start()

    @pl.loop(0, frames)
    def _(frame):
        for step in (1, 2, 3):
            near_copy(step, frame).start()

    for kind in range(5):
        mark_copy(kind).wait_recv()
    kinds[0] = marks[...]
    kinds[1] = mark_in[ACROSS]
    kinds[2] = jnp.concatenate([mark_in[kind][0:1] for kind in SIDES] + [marks[0:2]], axis=0)

    def chosen(rows, frame, mark):
        pick = wide(mark // 2 % 4)
        value = features[frame, rows]
        for step in (1, 2, 3):
            value = jnp.where(pick == step, near[step - 1, frame, rows], value)
        return value

    def start_swap(frame):
        for step in (1, 2, 3):
            near_copy(step, frame).wait_recv()
        for row in range(2):
            swap_out[frame, row * 8 : row * 8 + 8] = chosen(pl.ds(row * 8, 8), frame, kinds[0])
        swap_out[frame, 16:24] = chosen(pl.ds(pl.multiple_of(facing * 8, 8), 8), frame, kinds[1])
        for place, source in enumerate((7, 15, 0, 8, facing * 8 + 7, facing * 8)):
            mark = kinds[2, place : place + 1]
            swap_out[frame, 24 + place : 25 + place] = chosen(pl.ds(source, 1), frame, mark)
        swap_copy(frame).start()

    def start_core(frame):
        swap_copy(frame).wait_recv()
        for part, kind in enumerate((0, 0, 1, 2)):
            rows = slice(part * 8, part * 8 + 8)
            crossed = wide(kinds[kind]) // 8 == 1
            core_out[frame, rows] = jnp.where(crossed, swap_in[frame, rows], swap_out[frame, rows])
        core_copy(frame).start()

    def start_halo(frame):
        core_copy(frame).wait_recv()
        for part, kind in enumerate((0, 0, 1, 2)):
            rows = slice(part * 8, part * 8 + 8)
            crossed = wide(kinds[kind]) % 2 == 1
            value = jnp.where(crossed, core_in[frame, rows], core_out[frame, rows])
            if part < 2:
                block[frame, rows] = value
            else:
                halo[frame, part * 8 - 16 : part * 8 - 8] = value
        for kind in range(5):
            halo_copy(kind, frame).start()

    def start_norms():
        @pl.loop(1, 16)
        def _(other):
            sums_copy(other).wait_recv()

        value = sums[...]
        for other in range(1, 16):
            value = value + sums_in[other]
        value = group_sums(value) / (length.astype(F32) * 4096.0)
        mean = value[0:4]
        norms[0:4] = mean
        norms[4:8] = 1.0 / jnp.sqrt(value[4:8] - mean * mean + 1e-6)

        @pl.loop(1, 16)
        def _(other):
            norms_copy(other).start()

    @pl.loop(0, LOOPED)
    def _(step):
        start_swap(step)

        @pl.when(step >= CORE_AFTER)
        def _():
            start_core(step - CORE_AFTER)

        @pl.when(step >= HALO_AFTER)
        def _():
            start_halo(step - HALO_AFTER)

        @pl.when(step == 0)
        def _():
            loads[1].wait()
            loads[2].wait()

        @pl.when(step < 4)
        def _():
            @pl.loop(0, 6)
            def _(piece):
                prepare_time(step * 6 + piece, time_raw, time)

            @pl.loop(0, 4)
            def _(piece):
                prepare_space(step * 4 + piece, space_raw, space)

        @pl.when(step == 1)
        def _():
            start_norms()

    @pl.loop(1, 16)
    def _(other):
        norms_copy(other).wait_recv()

    for load in loads[3:]:
        load.wait()
    value = norms[...]
    for other in range(1, 16):
        value = jnp.where(marks[...] == other, norms_in[other], value)
    mean, scale = (
        jnp.concatenate([value[row + i : row + i + 1] for i in range(4)], axis=1) for row in (0, 4)
    )
    number = lambda flag: flag.astype(F32)
    upper, has_left, has_right = number(tile < 8), number(tile % 8 != 0), number(tile % 8 != 7)
    keep = lengths[grp ^ offsets[0]]

    def store(first, count):
        rows = pl.ds(first * 2, count * 2)
        return pltpu.make_async_copy(out.at[rows], result.at[rows], store_sem.at[first])

    def compute():
        first = 0
        for count in CHUNKS:
            for frame in range(first, first + count):
                for kind in range(5):
                    halo_copy(kind, frame).wait_recv()
            normalize(first, count, block, mean, scale, gain[...], bias[...], act)
            yield
            yield from decode(
                first, count, keep, upper, has_left, has_right, act, time, time_bias, space, space_bias,
                temporal, ops, stage, out,
            )
            store(first, count).start()
            first += count

    def transfers():
        for step in range(LOOPED, frames + HALO_AFTER):
            if step < frames:
                start_swap(step)
                yield
            if step < frames + CORE_AFTER:
                start_core(step - CORE_AFTER)
                yield
            start_halo(step - HALO_AFTER)
            yield

    work, moves = compute(), transfers()
    for _ in moves:
        next(work, None)
    for _ in work:
        pass

    first = 0
    for count in CHUNKS:
        store(first, count).wait()
        first += count
    for kind in range(5):
        mark_copy(kind).wait_send()

    @pl.loop(1, 16)
    def _(other):
        sums_copy(other).wait_send()
        norms_copy(other).wait_send()

    @pl.loop(0, frames)
    def _(frame):
        for step in (1, 2, 3):
            near_copy(step, frame).wait_send()
        swap_copy(frame).wait_send()
        core_copy(frame).wait_send()
        for kind in range(5):
            halo_copy(kind, frame).wait_send()


def decoded(offsets, lengths, features, gain, bias, time_weight, time_bias, space_weight, space_bias):
    frames = features.shape[0]
    scalars, anywhere = pl.BlockSpec(memory_space=pltpu.SMEM), pl.BlockSpec(memory_space=pl.ANY)
    sems = lambda *shape: [[pltpu.SemaphoreType.DMA(shape)] * 2]
    buffer = lambda *shape, kind=F32: pltpu.VMEM(shape, kind)
    most = max(CHUNKS)
    arrays = (features, gain, bias, time_weight, time_bias, space_weight, space_bias)
    return pl.pallas_call(
        kernel,
        out_shape=jax.ShapeDtypeStruct((2 * frames, 4, 16, 256), F32),
        in_specs=[scalars, scalars] + [anywhere] * 7,
        out_specs=anywhere,
        scratch_shapes=[buffer(*array.shape) for array in arrays]
        + [buffer(3, frames, 16, 512)]
        + [buffer(frames, 32, 512)] * 4
        + [buffer(frames, 16, 512), buffer(frames, 32, 512)]
        + [buffer(*shape, kind=jnp.int32) for shape in ((8, 128), (5, 8, 128), (3, 8, 128))]
        + [buffer(8, 128), buffer(16, 8, 128)] * 2
        + [buffer(2, *time_weight.shape, kind=BF16), buffer(2, 9, 512, 256, kind=BF16)]
        + [buffer(2, frames + 2, 32, 512, kind=BF16), buffer(most * 32, 1024), buffer(9, 2, most * 32, 512, kind=BF16)]
        + [buffer(2, most * 2, 4, 16, 128), buffer(2 * frames, 4, 16, 256)]
        + sems(3, frames) + sems(frames) * 2 + sems(5, frames) + sems(5) + sems(16) * 2
        + [pltpu.SemaphoreType.DMA((len(arrays),)), pltpu.SemaphoreType.DMA((frames,))],
        compiler_params=pltpu.CompilerParams(
            collective_id=0, has_side_effects=True, vmem_limit_bytes=58 * 2**20
        ),
    )(offsets, lengths, *arrays)


def on_device(features, lengths, offsets, norm_gain, norm_bias, time_weight, time_bias, space_weight, space_bias):
    frames, channels = features.shape[2], features.shape[-1]
    row = lambda array: array.reshape(1, -1)
    result = decoded(
        offsets, lengths, features.reshape(frames, 16, channels), row(norm_gain), row(norm_bias),
        time_weight, row(time_bias), space_weight, row(space_bias),
    )
    return result[None, None]


def solution(mesh):
    in_specs = (P("grp", "tile", None, None, None, None), P(), P("tile"), P(), P(), P(), P(), P(), P())
    out_specs = P("grp", "tile", None, None, None, None)
    return jax.shard_map(on_device, mesh=mesh, in_specs=in_specs, out_specs=out_specs, check_vma=False)
```

```python
import jax
import jax.numpy as jnp
from jax import lax
from jax.experimental import pallas as pl
from jax.experimental.pallas import tpu as pltpu
from jax.sharding import PartitionSpec as P

F32, BF16 = jnp.float32, jnp.bfloat16


def split(value):
    high = value.astype(BF16)
    return high, (value - high.astype(F32)).astype(BF16)


def prepare_time(step, raw, both):
    rows = 64
    depth = raw.shape[1]
    tap = step // (depth // rows)
    at = pl.ds(pl.multiple_of(step % (depth // rows) * rows, rows), rows)
    both[0, tap, at], both[1, tap, at] = split(raw[tap, at])


def prepare_space(step, raw, both):
    rows = 32
    at = pl.ds(pl.multiple_of(step * rows, rows), rows)
    kernel = [[raw[a, b, at] for b in range(3)] for a in range(3)]
    by_row = [kernel[0], [kernel[0][b] + kernel[1][b] + kernel[2][b] for b in range(3)], kernel[2]]
    for a in range(3):
        one = by_row[a]
        for b, value in enumerate((one[0], one[0] + one[1] + one[2], one[2])):
            both[0, a * 3 + b, at], both[1, a * 3 + b, at] = split(value)


def normalize(first, count, block, mean, scale, gain, bias, act):
    for frame in range(first, first + count):
        inner = (block[frame] - mean) * scale * gain + bias
        inner = inner / (1.0 + jnp.exp(-inner))
        act[0, frame + 2], act[1, frame + 2] = split(inner)


def decode(first, frames, keep, upper, has_left, has_right, act, time, time_bias, space, space_bias, temporal, ops, stage, out):
    rows, depth = frames * 32, act.shape[-1]
    both, high = [], []
    for tap in range(3):
        at = pl.ds(first + tap, frames)
        both.append(act[:, at].reshape(2 * rows, depth))
        high.append(act[0, at].reshape(rows, depth))
    weights = time.reshape(2, 3 * depth, 2 * depth)
    product = jnp.dot(jnp.concatenate(both, axis=1), weights[0], preferred_element_type=F32)
    yield
    rest = jnp.dot(jnp.concatenate(high, axis=1), weights[1], preferred_element_type=F32)
    temporal[0:rows] = product[:rows] + product[rows:] + rest + time_bias[...]
    yield
    place = lax.broadcasted_iota(jnp.int32, (8, depth), 0)
    for frame in range(frames):
        for half in range(2):
            lanes = slice(half * depth, half * depth + depth)
            block = lambda i: temporal[frame * 32 + i * 8 : frame * 32 + i * 8 + 8, lanes]
            row0, row1, across, side = block(0), block(1), block(2), block(3)
            columns = []
            for row, left, right in ((row0, 0, 2), (row1, 1, 3), (across, 4, 5)):
                before = jnp.where(place == 0, side[left : left + 1] * has_left, pltpu.roll(row, 1, 0))
                after = jnp.where(place == 7, side[right : right + 1] * has_right, pltpu.roll(row, 7, 0))
                columns.append((before - row, row, after - row))
            start = (frame * 2 + half) * 16
            for b in range(3):
                row0, row1, across = columns[0][b], columns[1][b], columns[2][b]
                above, below = across * (1.0 - upper), across * upper
                for a, value in enumerate((
                    jnp.concatenate([above - row0, row0 - row1], axis=0),
                    jnp.concatenate([row0, row1], axis=0),
                    jnp.concatenate([row1 - row0, below - row1], axis=0),
                )):
                    at = pl.ds(start, 16)
                    ops[a * 3 + b, 0, at], ops[a * 3 + b, 1, at] = split(value)
        yield
    parts = []
    for k in range(9):
        product = jnp.dot(ops[k, :, 0:rows].reshape(2 * rows, depth), space[0, k], preferred_element_type=F32)
        product = product[:rows] + product[rows:]
        parts.append(product + jnp.dot(ops[k, 0, 0:rows], space[1, k], preferred_element_type=F32))
        if k % 3 == 2:
            yield
    for up in range(2):
        base = [parts[6 * up + b] + parts[3 + b] for b in range(3)]
        for side in range(2):
            value = base[1] + base[2 * side] + space_bias[...]
            for frame in range(frames):
                for half in range(2):
                    start = (frame * 2 + half) * 16
                    for row in range(2):
                        piece = value[start + row * 8 : start + row * 8 + 8]
                        for lane in range(2):
                            stage[lane, frame * 2 + half, row * 2 + up, pl.ds(side, 8, stride=2), :] = piece[:, lane * 128 : lane * 128 + 128]
    yield
    for frame in range(frames):
        valid = (first + frame) < keep
        for half in range(2):
            for row in range(4):
                piece = jnp.concatenate([stage[lane, frame * 2 + half, row] for lane in range(2)], axis=1)
                out[(first + frame) * 2 + half, row] = jnp.where(valid, piece, 0.0)
    yield


MESH = pl.DeviceIdType.MESH
ACROSS, RIGHT, LEFT, ACROSS_RIGHT, ACROSS_LEFT = range(5)
MIRROR = (ACROSS, LEFT, RIGHT, ACROSS_LEFT, ACROSS_RIGHT)
SIDES = (RIGHT, RIGHT, LEFT, LEFT, ACROSS_RIGHT, ACROSS_LEFT)
PIECES = ((0, 8, 16), (8, 2, 24), (10, 2, 26), (12, 1, 28), (13, 1, 29))
SENT = 32


def wide(value, times=4):
    return jnp.concatenate([value] * times, axis=-1)


def group_sums(value):
    lane = lax.broadcasted_iota(jnp.int32, value.shape, 1)
    for step in (1, 2, 4, 8):
        ahead, behind = pltpu.roll(value, 128 - step, 1), pltpu.roll(value, step, 1)
        value = value + jnp.where(lane & step == 0, ahead, behind)
    return value


def tile_neighbours(tile):
    column, row = tile % 8, tile // 8
    right, left = (column + 1) % 8, (column + 7) % 8
    own, other = row * 8, (1 - row) * 8
    return other + column, own + right, own + left, other + right, other + left


CORE_AFTER, HALO_AFTER = 3, 4
CHUNKS = (4, 3, 2)
LOOPED = 9


def kernel(
    offsets, lengths, raw_features, gain_in, bias_in, time_in, time_bias_in, space_in, space_bias_in, result,
    features, gain, bias, time_raw, time_bias, space_raw, space_bias,
    near, swap_out, swap_in, core_out, core_in, halo, block,
    marks, mark_in, kinds, sums, sums_in, norms, norms_in,
    time, space, act, temporal, ops, stage, out,
    near_sem, swap_sem, core_sem, halo_sem, mark_sem, sums_sem, norms_sem, load_sem, store_sem,
):
    frames = features.shape[0]
    grp, tile = lax.axis_index("grp"), lax.axis_index("tile")
    neighbours = tile_neighbours(tile)
    facing = 1 - tile // 8

    loads = [
        pltpu.make_async_copy(source, target, load_sem.at[at])
        for at, (source, target) in enumerate((
            (raw_features, features), (time_in, time_raw), (space_in, space_raw), (gain_in, gain),
            (bias_in, bias), (time_bias_in, time_bias), (space_bias_in, space_bias),
        ))
    ]
    for load in loads:
        load.start()

    def send(source, target, sems, at, device):
        out_sem, in_sem = sems
        return pltpu.make_async_remote_copy(
            src_ref=source, dst_ref=target, send_sem=out_sem.at[at], recv_sem=in_sem.at[at],
            device_id=device, device_id_type=MESH,
        )

    def near_copy(step, frame):
        return send(raw_features.at[frame], near.at[step - 1, frame], near_sem, (step - 1, frame), (grp ^ (step * 2), tile))

    def swap_copy(frame):
        rows = pl.ds(0, SENT)
        return send(swap_out.at[frame, rows], swap_in.at[frame, rows], swap_sem, frame, (grp ^ 8, tile))

    def core_copy(frame):
        rows = pl.ds(0, SENT)
        return send(core_out.at[frame, rows], core_in.at[frame, rows], core_sem, frame, (grp ^ 1, tile))

    def halo_copy(kind, frame):
        start, count, land = PIECES[kind]
        return send(
            halo.at[frame, pl.ds(start, count)], block.at[frame, pl.ds(land, count)],
            halo_sem, (kind, frame), (grp, neighbours[kind]),
        )

    def mark_copy(kind):
        return send(marks, mark_in.at[MIRROR[kind]], mark_sem, MIRROR[kind], (grp, neighbours[kind]))

    def sums_copy(step):
        return send(sums, sums_in.at[step], sums_sem, step, (grp, (tile + step) % 16))

    def norms_copy(step):
        return send(norms, norms_in.at[step], norms_sem, step, (grp ^ step, tile))

    barrier = pltpu.get_barrier_semaphore()

    @pl.loop(1, 16)
    def _(step):
        pl.semaphore_signal(barrier, inc=1, device_id=(grp, (tile + step) % 16), device_id_type=MESH)
        pl.semaphore_signal(barrier, inc=1, device_id=(grp ^ step, tile), device_id_type=MESH)

    marks[...] = jnp.full(marks.shape, offsets[0], jnp.int32)
    act[:, 0:2] = jnp.zeros((2, 2, 32, 512), BF16)
    pl.semaphore_wait(barrier, 30)
    for kind in range(5):
        mark_copy(kind).start()

    @pl.loop(0, frames)
    def _(frame):
        for step in (1, 2, 3):
            near_copy(step, frame).start()

    length = lengths[grp]
    loads[0].wait()
    total, squares = jnp.zeros((8, 512), F32), jnp.zeros((8, 512), F32)
    for frame in range(frames):
        for row in range(2):
            value = jnp.where(frame < length, features[frame, row * 8 : row * 8 + 8], 0.0)
            total, squares = total + value, squares + value * value
    total, squares = jnp.sum(total, axis=0, keepdims=True), jnp.sum(squares, axis=0, keepdims=True)
    for part in range(4):
        sums[part : part + 1] = total[:, part * 128 : part * 128 + 128]
        sums[part + 4 : part + 5] = squares[:, part * 128 : part * 128 + 128]

    @pl.loop(1, 16)
    def _(step):
        sums_copy(step).start()

    for kind in range(5):
        mark_copy(kind).wait_recv()
    kinds[0] = marks[...]
    kinds[1] = mark_in[ACROSS]
    kinds[2] = jnp.concatenate([mark_in[kind][0:1] for kind in SIDES] + [marks[0:2]], axis=0)

    def chosen(rows, frame, mark):
        pick = wide(mark // 2 % 4)
        value = features[frame, rows]
        for step in (1, 2, 3):
            value = jnp.where(pick == step, near[step - 1, frame, rows], value)
        return value

    def start_swap(frame):
        for step in (1, 2, 3):
            near_copy(step, frame).wait_recv()
        for row in range(2):
            swap_out[frame, row * 8 : row * 8 + 8] = chosen(pl.ds(row * 8, 8), frame, kinds[0])
        swap_out[frame, 16:24] = chosen(pl.ds(pl.multiple_of(facing * 8, 8), 8), frame, kinds[1])
        for place, source in enumerate((7, 15, 0, 8, facing * 8 + 7, facing * 8)):
            mark = kinds[2, place : place + 1]
            swap_out[frame, 24 + place : 25 + place] = chosen(pl.ds(source, 1), frame, mark)
        swap_copy(frame).start()

    def start_core(frame):
        swap_copy(frame).wait_recv()
        for part, kind in enumerate((0, 0, 1, 2)):
            rows = slice(part * 8, part * 8 + 8)
            crossed = wide(kinds[kind]) // 8 == 1
            core_out[frame, rows] = jnp.where(crossed, swap_in[frame, rows], swap_out[frame, rows])
        core_copy(frame).start()

    def start_halo(frame):
        core_copy(frame).wait_recv()
        for part, kind in enumerate((0, 0, 1, 2)):
            rows = slice(part * 8, part * 8 + 8)
            crossed = wide(kinds[kind]) % 2 == 1
            value = jnp.where(crossed, core_in[frame, rows], core_out[frame, rows])
            if part < 2:
                block[frame, rows] = value
            else:
                halo[frame, part * 8 - 16 : part * 8 - 8] = value
        for kind in range(5):
            halo_copy(kind, frame).start()

    def start_norms():
        @pl.loop(1, 16)
        def _(other):
            sums_copy(other).wait_recv()

        value = sums[...]
        for other in range(1, 16):
            value = value + sums_in[other]
        value = group_sums(value) / (length.astype(F32) * 4096.0)
        mean = value[0:4]
        norms[0:4] = mean
        norms[4:8] = 1.0 / jnp.sqrt(value[4:8] - mean * mean + 1e-6)

        @pl.loop(1, 16)
        def _(other):
            norms_copy(other).start()

    @pl.loop(0, LOOPED)
    def _(step):
        start_swap(step)

        @pl.when(step >= CORE_AFTER)
        def _():
            start_core(step - CORE_AFTER)

        @pl.when(step >= HALO_AFTER)
        def _():
            start_halo(step - HALO_AFTER)

        @pl.when(step == 0)
        def _():
            loads[1].wait()
            loads[2].wait()

        @pl.when(step < 4)
        def _():
            @pl.loop(0, 6)
            def _(piece):
                prepare_time(step * 6 + piece, time_raw, time)

            @pl.loop(0, 4)
            def _(piece):
                prepare_space(step * 4 + piece, space_raw, space)

        @pl.when(step == 1)
        def _():
            start_norms()

    @pl.loop(1, 16)
    def _(other):
        norms_copy(other).wait_recv()

    for load in loads[3:]:
        load.wait()
    value = norms[...]
    for other in range(1, 16):
        value = jnp.where(marks[...] == other, norms_in[other], value)
    mean, scale = (
        jnp.concatenate([value[row + i : row + i + 1] for i in range(4)], axis=1) for row in (0, 4)
    )
    number = lambda flag: flag.astype(F32)
    upper, has_left, has_right = number(tile < 8), number(tile % 8 != 0), number(tile % 8 != 7)
    keep = lengths[grp ^ offsets[0]]

    def store(first, count):
        rows = pl.ds(first * 2, count * 2)
        return pltpu.make_async_copy(out.at[rows], result.at[rows], store_sem.at[first])

    def compute():
        first = 0
        for count in CHUNKS:
            for frame in range(first, first + count):
                for kind in range(5):
                    halo_copy(kind, frame).wait_recv()
            normalize(first, count, block, mean, scale, gain[...], bias[...], act)
            yield
            yield from decode(
                first, count, keep, upper, has_left, has_right, act, time, time_bias, space, space_bias,
                temporal, ops, stage, out,
            )
            store(first, count).start()
            first += count

    def transfers():
        for step in range(LOOPED, frames + HALO_AFTER):
            if step < frames:
                start_swap(step)
                yield
            if step < frames + CORE_AFTER:
                start_core(step - CORE_AFTER)
                yield
            start_halo(step - HALO_AFTER)
            yield

    work, moves = compute(), transfers()
    for _ in moves:
        next(work, None)
    for _ in work:
        pass

    first = 0
    for count in CHUNKS:
        store(first, count).wait()
        first += count
    for kind in range(5):
        mark_copy(kind).wait_send()

    @pl.loop(1, 16)
    def _(other):
        sums_copy(other).wait_send()
        norms_copy(other).wait_send()

    @pl.loop(0, frames)
    def _(frame):
        for step in (1, 2, 3):
            near_copy(step, frame).wait_send()
        swap_copy(frame).wait_send()
        core_copy(frame).wait_send()
        for kind in range(5):
            halo_copy(kind, frame).wait_send()


def decoded(offsets, lengths, features, gain, bias, time_weight, time_bias, space_weight, space_bias):
    frames = features.shape[0]
    scalars, anywhere = pl.BlockSpec(memory_space=pltpu.SMEM), pl.BlockSpec(memory_space=pl.ANY)
    sems = lambda *shape: [[pltpu.SemaphoreType.DMA(shape)] * 2]
    buffer = lambda *shape, kind=F32: pltpu.VMEM(shape, kind)
    most = max(CHUNKS)
    arrays = (features, gain, bias, time_weight, time_bias, space_weight, space_bias)
    return pl.pallas_call(
        kernel,
        out_shape=jax.ShapeDtypeStruct((2 * frames, 4, 16, 256), F32),
        in_specs=[scalars, scalars] + [anywhere] * 7,
        out_specs=anywhere,
        scratch_shapes=[buffer(*array.shape) for array in arrays]
        + [buffer(3, frames, 16, 512)]
        + [buffer(frames, 32, 512)] * 4
        + [buffer(frames, 16, 512), buffer(frames, 32, 512)]
        + [buffer(*shape, kind=jnp.int32) for shape in ((8, 128), (5, 8, 128), (3, 8, 128))]
        + [buffer(8, 128), buffer(16, 8, 128)] * 2
        + [buffer(2, *time_weight.shape, kind=BF16), buffer(2, 9, 512, 256, kind=BF16)]
        + [buffer(2, frames + 2, 32, 512, kind=BF16), buffer(most * 32, 1024), buffer(9, 2, most * 32, 512, kind=BF16)]
        + [buffer(2, most * 2, 4, 16, 128), buffer(2 * frames, 4, 16, 256)]
        + sems(3, frames) + sems(frames) * 2 + sems(5, frames) + sems(5) + sems(16) * 2
        + [pltpu.SemaphoreType.DMA((len(arrays),)), pltpu.SemaphoreType.DMA((frames,))],
        compiler_params=pltpu.CompilerParams(
            collective_id=0, has_side_effects=True, vmem_limit_bytes=58 * 2**20
        ),
    )(offsets, lengths, *arrays)


def on_device(features, lengths, offsets, norm_gain, norm_bias, time_weight, time_bias, space_weight, space_bias):
    frames, channels = features.shape[2], features.shape[-1]
    row = lambda array: array.reshape(1, -1)
    result = decoded(
        offsets, lengths, features.reshape(frames, 16, channels), row(norm_gain), row(norm_bias),
        time_weight, row(time_bias), space_weight, row(space_bias),
    )
    return result[None, None]


def solution(mesh):
    in_specs = (P("grp", "tile", None, None, None, None), P(), P("tile"), P(), P(), P(), P(), P(), P())
    out_specs = P("grp", "tile", None, None, None, None)
    return jax.shard_map(on_device, mesh=mesh, in_specs=in_specs, out_specs=out_specs, check_vma=False)
```

```python
import jax
import jax.numpy as jnp
from jax import lax
from jax.experimental import pallas as pl
from jax.experimental.pallas import tpu as pltpu
from jax.sharding import PartitionSpec as P

F32, BF16 = jnp.float32, jnp.bfloat16


def split(value):
    high = value.astype(BF16)
    return high, (value - high.astype(F32)).astype(BF16)


def prepare_time(step, raw, both):
    rows = 64
    depth = raw.shape[1]
    tap = step // (depth // rows)
    at = pl.ds(pl.multiple_of(step % (depth // rows) * rows, rows), rows)
    both[0, tap, at], both[1, tap, at] = split(raw[tap, at])


def prepare_space(step, raw, both):
    rows = 32
    at = pl.ds(pl.multiple_of(step * rows, rows), rows)
    kernel = [[raw[a, b, at] for b in range(3)] for a in range(3)]
    by_row = [kernel[0], [kernel[0][b] + kernel[1][b] + kernel[2][b] for b in range(3)], kernel[2]]
    for a in range(3):
        one = by_row[a]
        for b, value in enumerate((one[0], one[0] + one[1] + one[2], one[2])):
            both[0, a * 3 + b, at], both[1, a * 3 + b, at] = split(value)


def normalize(first, count, block, mean, scale, gain, bias, act):
    for frame in range(first, first + count):
        inner = (block[frame] - mean) * scale * gain + bias
        inner = inner / (1.0 + jnp.exp(-inner))
        act[0, frame + 2], act[1, frame + 2] = split(inner)


def decode(first, frames, keep, facing, upper, has_left, has_right, act, time, time_bias, space, space_bias, temporal, ops, stage, out):
    rows, depth = frames * 32, act.shape[-1]
    both, high = [], []
    for tap in range(3):
        at = pl.ds(first + tap, frames)
        both.append(act[:, at].reshape(2 * rows, depth))
        high.append(act[0, at].reshape(rows, depth))
    weights = time.reshape(2, 3 * depth, 2 * depth)
    product = jnp.dot(jnp.concatenate(both, axis=1), weights[0], preferred_element_type=F32)
    yield
    rest = jnp.dot(jnp.concatenate(high, axis=1), weights[1], preferred_element_type=F32)
    temporal[0:rows] = product[:rows] + product[rows:] + rest + time_bias[...]
    yield
    place = lax.broadcasted_iota(jnp.int32, (8, depth), 0)
    for frame in range(frames):
        for half in range(2):
            lanes = slice(half * depth, half * depth + depth)
            block = lambda i: temporal[pl.ds(pl.multiple_of(frame * 32 + i * 8, 8), 8), lanes]
            side = lambda i: temporal[pl.ds(frame * 32 + 24 + i, 1), lanes]
            other = 1 - facing
            columns = []
            for row, left, right in (
                (block(facing), facing, 2 + facing), (block(other), other, 2 + other), (block(2), 4, 5),
            ):
                before = jnp.where(place == 0, side(left) * has_left, pltpu.roll(row, 1, 0))
                after = jnp.where(place == 7, side(right) * has_right, pltpu.roll(row, 7, 0))
                columns.append((before - row, row, after - row))
            start = (frame * 2 + half) * 16
            for b in range(3):
                row0, row1, across = columns[0][b], columns[1][b], columns[2][b]
                above, below = across * (1.0 - upper), across * upper
                for a, value in enumerate((
                    jnp.concatenate([above - row0, row0 - row1], axis=0),
                    jnp.concatenate([row0, row1], axis=0),
                    jnp.concatenate([row1 - row0, below - row1], axis=0),
                )):
                    at = pl.ds(start, 16)
                    ops[a * 3 + b, 0, at], ops[a * 3 + b, 1, at] = split(value)
        yield
    parts = []
    for k in range(9):
        product = jnp.dot(ops[k, :, 0:rows].reshape(2 * rows, depth), space[0, k], preferred_element_type=F32)
        product = product[:rows] + product[rows:]
        parts.append(product + jnp.dot(ops[k, 0, 0:rows], space[1, k], preferred_element_type=F32))
        if k % 3 == 2:
            yield
    for up in range(2):
        base = [parts[6 * up + b] + parts[3 + b] for b in range(3)]
        for side in range(2):
            value = base[1] + base[2 * side] + space_bias[...]
            for frame in range(frames):
                for half in range(2):
                    start = (frame * 2 + half) * 16
                    for row in range(2):
                        piece = value[start + row * 8 : start + row * 8 + 8]
                        for lane in range(2):
                            stage[lane, frame * 2 + half, row * 2 + up, pl.ds(side, 8, stride=2), :] = piece[:, lane * 128 : lane * 128 + 128]
    yield
    for frame in range(frames):
        valid = (first + frame) < keep
        for half in range(2):
            for row in range(4):
                piece = jnp.concatenate([stage[lane, frame * 2 + half, row] for lane in range(2)], axis=1)
                out[(first + frame) * 2 + half, row] = jnp.where(valid, piece, 0.0)
    yield


MESH = pl.DeviceIdType.MESH
ACROSS, RIGHT, LEFT, ACROSS_RIGHT, ACROSS_LEFT = range(5)
MIRROR = (ACROSS, LEFT, RIGHT, ACROSS_LEFT, ACROSS_RIGHT)
DIAGONALS, SIDES = (ACROSS_RIGHT, ACROSS_LEFT), (RIGHT, RIGHT, LEFT, LEFT)
PIECES = ((0, 8, 16), (16, 2, 24), (18, 2, 26), (8, 1, 28), (9, 1, 29))
VERTICAL, ENDS, FACING, SIDE, OTHER = range(5)
PLACES = ((0, 8), (8, 2), (16, 8), (24, 4), (32, 8))


def wide(value, times=4):
    return jnp.concatenate([value] * times, axis=-1)


def group_sums(value):
    lane = lax.broadcasted_iota(jnp.int32, value.shape, 1)
    for step in (1, 2, 4, 8):
        ahead, behind = pltpu.roll(value, 128 - step, 1), pltpu.roll(value, step, 1)
        value = value + jnp.where(lane & step == 0, ahead, behind)
    return value


def tile_neighbours(tile):
    column, row = tile % 8, tile // 8
    right, left = (column + 1) % 8, (column + 7) % 8
    own, other = row * 8, (1 - row) * 8
    return other + column, own + right, own + left, other + right, other + left


MARKS_AT, OWN_AFTER, CORE_AFTER, HALO_AFTER = 4, 2, 8, 10
CHUNKS = (3, 3, 3)
SIDE_AFTER, LEAD = 6, 6
NORMS_AT = 6


def kernel(
    offsets, lengths, raw_features, gain_in, bias_in, time_in, time_bias_in, space_in, space_bias_in, result,
    features, gain, bias, time_raw, time_bias, space_raw, space_bias,
    near, swap_out, swap_in, core_out, core_in, halo, block,
    marks, mark_in, kinds, sums, sums_in, norms, norms_in,
    time, space, act, temporal, ops, stage, out,
    near_sem, swap_sem, core_sem, halo_sem, mark_sem, sums_sem, norms_sem, load_sem, store_sem,
):
    frames = raw_features.shape[0]
    grp, tile = lax.axis_index("grp"), lax.axis_index("tile")
    neighbours = tile_neighbours(tile)
    facing = 1 - tile // 8

    loads = [
        pltpu.make_async_copy(source, target, load_sem.at[at])
        for at, (source, target) in enumerate((
            (raw_features.at[:, pl.ds(pl.multiple_of(facing * 8, 8), 8)], features.at[0]), (time_in, time_raw), (space_in, space_raw), (gain_in, gain),
            (bias_in, bias), (time_bias_in, time_bias), (space_bias_in, space_bias),
            (raw_features.at[:, pl.ds(pl.multiple_of(8 - facing * 8, 8), 8)], features.at[1]),
        ))
    ]
    for load in loads[7:] + loads[:7]:
        load.start()

    def send(source, target, sems, at, device):
        out_sem, in_sem = sems
        return pltpu.make_async_remote_copy(
            src_ref=source, dst_ref=target, send_sem=out_sem.at[at], recv_sem=in_sem.at[at],
            device_id=device, device_id_type=MESH,
        )

    def near_copy(step, half, frame):
        start = facing * 8 if half == 0 else 8 - facing * 8
        source = raw_features.at[frame, pl.ds(pl.multiple_of(start, 8), 8)]
        return send(source, near.at[step - 1, half, frame], near_sem, (step - 1, half, frame), (grp ^ (step * 2), tile))

    def swap_copy(part, frame):
        rows = pl.ds(*PLACES[part])
        return send(swap_out.at[frame, rows], swap_in.at[frame, rows], swap_sem, (part, frame), (grp ^ 8, tile))

    def core_copy(part, frame):
        rows = pl.ds(*PLACES[part])
        return send(core_out.at[frame, rows], core_in.at[frame, rows], core_sem, (part, frame), (grp ^ 1, tile))

    def halo_copy(kind, frame):
        start, count, land = PIECES[kind]
        return send(
            halo.at[frame, pl.ds(start, count)], block.at[frame, pl.ds(land, count)],
            halo_sem, (kind, frame), (grp, neighbours[kind]),
        )

    def mark_copy(kind):
        return send(marks, mark_in.at[MIRROR[kind]], mark_sem, MIRROR[kind], (grp, neighbours[kind]))

    def sums_copy(step):
        return send(sums, sums_in.at[step], sums_sem, step, (grp, (tile + step) % 16))

    def norms_copy(step):
        return send(norms, norms_in.at[step], norms_sem, step, (grp ^ step, tile))

    barrier = pltpu.get_barrier_semaphore()

    @pl.loop(1, 16)
    def _(step):
        pl.semaphore_signal(barrier, inc=1, device_id=(grp, (tile + step) % 16), device_id_type=MESH)
        pl.semaphore_signal(barrier, inc=1, device_id=(grp ^ step, tile), device_id_type=MESH)

    marks[...] = jnp.full(marks.shape, offsets[0], jnp.int32)
    act[:, 0:2] = jnp.zeros((2, 2, 32, 512), BF16)
    pl.semaphore_wait(barrier, 30)
    for kind in range(5):
        mark_copy(kind).start()

    @pl.loop(0, LEAD)
    def _(frame):
        for step in (1, 2, 3):
            near_copy(step, 0, frame).start()

    length = lengths[grp]
    loads[0].wait()
    loads[7].wait()
    total, squares = jnp.zeros((8, 512), F32), jnp.zeros((8, 512), F32)
    for frame in range(frames):
        for row in range(2):
            value = jnp.where(frame < length, features[row, frame], 0.0)
            total, squares = total + value, squares + value * value
    total, squares = jnp.sum(total, axis=0, keepdims=True), jnp.sum(squares, axis=0, keepdims=True)
    for part in range(4):
        sums[part : part + 1] = total[:, part * 128 : part * 128 + 128]
        sums[part + 4 : part + 5] = squares[:, part * 128 : part * 128 + 128]

    @pl.loop(1, 16)
    def _(step):
        sums_copy(step).start()

    kinds[0] = marks[...]

    def chosen(half, rows, frame, mark):
        pick = wide(mark // 2 % 4)
        value = features[half, frame, rows]
        for step in (1, 2, 3):
            value = jnp.where(pick == step, near[step - 1, half, frame, rows], value)
        return value

    def learn_marks():
        for kind in range(5):
            mark_copy(kind).wait_recv()
        kinds[1] = mark_in[ACROSS]
        for at, picked in ((2, DIAGONALS), (3, SIDES)):
            kinds[at] = jnp.concatenate([mark_in[kind][0:1] for kind in picked] + [marks[len(picked) :]], axis=0)

    def wait_near(half, frame):
        for step in (1, 2, 3):
            near_copy(step, half, frame).wait_recv()

    def swap_part(part, frame):
        start, count = PLACES[part]
        rows = pl.ds(0, 8)
        if part == VERTICAL:
            swap_out[frame, start : start + 8] = chosen(0, rows, frame, kinds[1])
        elif part in (FACING, OTHER):
            swap_out[frame, start : start + 8] = chosen(int(part == OTHER), rows, frame, kinds[0])
        else:
            cells = ((0, 7), (0, 0)) if part == ENDS else ((0, 7), (1, 7), (0, 0), (1, 0))
            for place, (half, cell) in enumerate(cells):
                mark = kinds[2 if part == ENDS else 3, place : place + 1]
                swap_out[frame, start + place : start + place + 1] = chosen(half, pl.ds(cell, 1), frame, mark)
        swap_copy(part, frame).start()

    def mark_of(part):
        return wide(kinds[(1, 2, 0, 3, 0)[part]])

    def core_part(part, frame):
        swap_copy(part, frame).wait_recv()
        rows = slice(PLACES[part][0], PLACES[part][0] + 8)
        crossed = mark_of(part) // 8 == 1
        core_out[frame, rows] = jnp.where(crossed, swap_in[frame, rows], swap_out[frame, rows])
        core_copy(part, frame).start()

    def final(part, frame):
        core_copy(part, frame).wait_recv()
        rows = slice(PLACES[part][0], PLACES[part][0] + 8)
        return jnp.where(mark_of(part) % 2 == 1, core_in[frame, rows], core_out[frame, rows])

    def send_vertical(frame):
        for part, kinds_sent in ((VERTICAL, (ACROSS,)), (ENDS, DIAGONALS)):
            halo[frame, part * 8 : part * 8 + 8] = final(part, frame)
            for kind in kinds_sent:
                halo_copy(kind, frame).start()

    def send_sides(frame):
        halo[frame, 16:24] = final(SIDE, frame)
        for kind in (RIGHT, LEFT):
            halo_copy(kind, frame).start()

    def finish(frame):
        block[frame, 0:8] = final(FACING, frame)
        block[frame, 8:16] = final(OTHER, frame)

    def start_norms():
        @pl.loop(1, 16)
        def _(other):
            sums_copy(other).wait_recv()

        value = sums[...]
        for other in range(1, 16):
            value = value + sums_in[other]
        value = group_sums(value) / (length.astype(F32) * 4096.0)
        mean = value[0:4]
        norms[0:4] = mean
        norms[4:8] = 1.0 / jnp.sqrt(value[4:8] - mean * mean + 1e-6)

        @pl.loop(1, 16)
        def _(other):
            norms_copy(other).start()

    def swap_vertical(frame):
        swap_part(VERTICAL, frame)
        swap_part(ENDS, frame)

    def core_vertical(frame):
        core_part(VERTICAL, frame)
        core_part(ENDS, frame)

    def start_near(step):
        for half in range(2):
            @pl.when((step >= half * frames) & (step < half * frames + frames))
            def _():
                for other in (1, 2, 3):
                    near_copy(other, half, step - half * frames).start()

    @pl.loop(0, frames)
    def _(step):
        start_near(step + LEAD)
        wait_near(0, step)

        @pl.when(step < MARKS_AT)
        def _():
            swap_part(FACING, step)

        @pl.when(step == MARKS_AT)
        def _():
            learn_marks()
            for frame in range(MARKS_AT):
                swap_vertical(frame)

        @pl.when(step >= MARKS_AT)
        def _():
            swap_vertical(step)

        @pl.when(step >= MARKS_AT + OWN_AFTER)
        def _():
            swap_part(FACING, step - OWN_AFTER)

        @pl.when(step >= CORE_AFTER)
        def _():
            core_vertical(step - CORE_AFTER)

        @pl.when(step == 0)
        def _():
            loads[1].wait()
            loads[2].wait()

        @pl.when(step < 8)
        def _():
            for piece in range(3):
                prepare_time(step * 3 + piece, time_raw, time)
            for piece in range(2):
                prepare_space(step * 2 + piece, space_raw, space)

        @pl.when(step == NORMS_AT)
        def _():
            start_norms()

    @pl.loop(0, frames)
    def _(frame):
        step = frame + frames
        start_near(step + LEAD)
        wait_near(1, frame)
        swap_part(SIDE, frame)
        swap_part(OTHER, frame)

        @pl.when(frame < OWN_AFTER)
        def _():
            swap_part(FACING, step - OWN_AFTER)

        @pl.when(step < frames + CORE_AFTER)
        def _():
            core_vertical(step - CORE_AFTER)

        @pl.when(step >= HALO_AFTER)
        def _():
            send_vertical(step - HALO_AFTER)

        core_part(FACING, frame)

        @pl.when(frame >= SIDE_AFTER)
        def _():
            core_part(SIDE, frame - SIDE_AFTER)
            core_part(OTHER, frame - SIDE_AFTER)

        @pl.when(frame >= SIDE_AFTER + 1)
        def _():
            send_sides(frame - SIDE_AFTER - 1)

    @pl.loop(1, 16)
    def _(other):
        norms_copy(other).wait_recv()

    for load in loads[3:7]:
        load.wait()
    value = norms[...]
    for other in range(1, 16):
        value = jnp.where(marks[...] == other, norms_in[other], value)
    mean, scale = (
        jnp.concatenate([value[row + i : row + i + 1] for i in range(4)], axis=1) for row in (0, 4)
    )
    number = lambda flag: flag.astype(F32)
    upper, has_left, has_right = number(tile < 8), number(tile % 8 != 0), number(tile % 8 != 7)
    keep = lengths[grp ^ offsets[0]]

    def store(first, count):
        rows = pl.ds(first * 2, count * 2)
        return pltpu.make_async_copy(out.at[rows], result.at[rows], store_sem.at[first])

    def compute():
        first = 0
        for count in CHUNKS:
            for frame in range(first, first + count):
                for kind in range(5):
                    halo_copy(kind, frame).wait_recv()
            normalize(first, count, block, mean, scale, gain[...], bias[...], act)
            yield
            yield from decode(
                first, count, keep, facing, upper, has_left, has_right, act, time, time_bias, space, space_bias,
                temporal, ops, stage, out,
            )
            store(first, count).start()
            first += count

    def transfers():
        left = frames - SIDE_AFTER
        for frame in range(2 * frames - HALO_AFTER, frames):
            send_vertical(frame)
        for frame in range(left, left + 2):
            core_part(SIDE, frame)
            core_part(OTHER, frame)
            send_sides(frame - 1)
        for frame in range(left):
            finish(frame)
        yield
        for frame in range(left + 2, frames):
            core_part(SIDE, frame)
            core_part(OTHER, frame)
            send_sides(frame - 1)
            finish(frame - 2)
            yield
        send_sides(frames - 1)
        for frame in range(frames - 2, frames):
            finish(frame)

    work, moves = compute(), transfers()
    for _ in moves:
        next(work)
    for _ in work:
        pass

    first = 0
    for count in CHUNKS:
        store(first, count).wait()
        first += count
    for kind in range(5):
        mark_copy(kind).wait_send()

    @pl.loop(1, 16)
    def _(other):
        sums_copy(other).wait_send()
        norms_copy(other).wait_send()

    @pl.loop(0, frames)
    def _(frame):
        for half in range(2):
            for step in (1, 2, 3):
                near_copy(step, half, frame).wait_send()
        for part in range(5):
            swap_copy(part, frame).wait_send()
            core_copy(part, frame).wait_send()
        for kind in range(5):
            halo_copy(kind, frame).wait_send()


def decoded(offsets, lengths, features, gain, bias, time_weight, time_bias, space_weight, space_bias):
    frames = features.shape[0]
    scalars, anywhere = pl.BlockSpec(memory_space=pltpu.SMEM), pl.BlockSpec(memory_space=pl.ANY)
    sems = lambda *shape: [[pltpu.SemaphoreType.DMA(shape)] * 2]
    buffer = lambda *shape, kind=F32: pltpu.VMEM(shape, kind)
    most = max(CHUNKS)
    arrays = (features, gain, bias, time_weight, time_bias, space_weight, space_bias)
    return pl.pallas_call(
        kernel,
        out_shape=jax.ShapeDtypeStruct((2 * frames, 4, 16, 256), F32),
        in_specs=[scalars, scalars] + [anywhere] * 7,
        out_specs=anywhere,
        scratch_shapes=[buffer(2, frames, 8, 512)] + [buffer(*array.shape) for array in arrays[1:]]
        + [buffer(3, 2, frames, 8, 512)]
        + [buffer(frames, 40, 512)] * 4
        + [buffer(frames, 24, 512), buffer(frames, 32, 512)]
        + [buffer(*shape, kind=jnp.int32) for shape in ((8, 128), (5, 8, 128), (4, 8, 128))]
        + [buffer(8, 128), buffer(16, 8, 128)] * 2
        + [buffer(2, *time_weight.shape, kind=BF16), buffer(2, 9, 512, 256, kind=BF16)]
        + [buffer(2, frames + 2, 32, 512, kind=BF16), buffer(most * 32, 1024), buffer(9, 2, most * 32, 512, kind=BF16)]
        + [buffer(2, most * 2, 4, 16, 128), buffer(2 * frames, 4, 16, 256)]
        + sems(3, 2, frames) + sems(5, frames) * 3 + sems(5) + sems(16) * 2
        + [pltpu.SemaphoreType.DMA((len(arrays) + 1,)), pltpu.SemaphoreType.DMA((frames,))],
        compiler_params=pltpu.CompilerParams(
            collective_id=0, has_side_effects=True, vmem_limit_bytes=58 * 2**20
        ),
    )(offsets, lengths, *arrays)


def on_device(features, lengths, offsets, norm_gain, norm_bias, time_weight, time_bias, space_weight, space_bias):
    frames, channels = features.shape[2], features.shape[-1]
    row = lambda array: array.reshape(1, -1)
    result = decoded(
        offsets, lengths, features.reshape(frames, 16, channels), row(norm_gain), row(norm_bias),
        time_weight, row(time_bias), space_weight, row(space_bias),
    )
    return result[None, None]


def solution(mesh):
    in_specs = (P("grp", "tile", None, None, None, None), P(), P("tile"), P(), P(), P(), P(), P(), P())
    out_specs = P("grp", "tile", None, None, None, None)
    return jax.shard_map(on_device, mesh=mesh, in_specs=in_specs, out_specs=out_specs, check_vma=False)
```

```python
import jax
import jax.numpy as jnp
from jax import lax
from jax.experimental import pallas as pl
from jax.experimental.pallas import tpu as pltpu
from jax.sharding import PartitionSpec as P

F32, BF16 = jnp.float32, jnp.bfloat16


def split(value):
    high = value.astype(BF16)
    return high, (value - high.astype(F32)).astype(BF16)


def prepare_time(step, raw, both):
    rows = 64
    depth = raw.shape[1]
    tap = step // (depth // rows)
    at = pl.ds(pl.multiple_of(step % (depth // rows) * rows, rows), rows)
    both[0, tap, at], both[1, tap, at] = split(raw[tap, at])


def prepare_space(step, raw, both):
    rows = 32
    at = pl.ds(pl.multiple_of(step * rows, rows), rows)
    kernel = [[raw[a, b, at] for b in range(3)] for a in range(3)]
    by_row = [kernel[0], [kernel[0][b] + kernel[1][b] + kernel[2][b] for b in range(3)], kernel[2]]
    for a in range(3):
        one = by_row[a]
        for b, value in enumerate((one[0], one[0] + one[1] + one[2], one[2])):
            both[0, a * 3 + b, at], both[1, a * 3 + b, at] = split(value)


def normalize(first, count, block, mean, scale, gain, bias, act):
    for frame in range(first, first + count):
        inner = (block[frame] - mean) * scale * gain + bias
        inner = inner / (1.0 + jnp.exp(-inner))
        act[0, frame + 2], act[1, frame + 2] = split(inner)


def decode(first, frames, keep, facing, upper, has_left, has_right, act, time, time_bias, space, space_bias, temporal, ops, stage, out):
    rows, depth = frames * 32, act.shape[-1]
    both, high = [], []
    for tap in range(3):
        at = pl.ds(first + tap, frames)
        both.append(act[:, at].reshape(2 * rows, depth))
        high.append(act[0, at].reshape(rows, depth))
    weights = time.reshape(2, 3 * depth, 2 * depth)
    product = jnp.dot(jnp.concatenate(both, axis=1), weights[0], preferred_element_type=F32)
    yield
    rest = jnp.dot(jnp.concatenate(high, axis=1), weights[1], preferred_element_type=F32)
    temporal[0:rows] = product[:rows] + product[rows:] + rest + time_bias[...]
    yield
    place = lax.broadcasted_iota(jnp.int32, (8, depth), 0)
    for frame in range(frames):
        for half in range(2):
            lanes = slice(half * depth, half * depth + depth)
            block = lambda i: temporal[pl.ds(pl.multiple_of(frame * 32 + i * 8, 8), 8), lanes]
            side = lambda i: temporal[pl.ds(frame * 32 + 24 + i, 1), lanes]
            other = 1 - facing
            columns = []
            for row, left, right in (
                (block(facing), facing, 2 + facing), (block(other), other, 2 + other), (block(2), 4, 5),
            ):
                before = jnp.where(place == 0, jnp.where(has_left, side(left), 0.0), pltpu.roll(row, 1, 0))
                after = jnp.where(place == 7, jnp.where(has_right, side(right), 0.0), pltpu.roll(row, 7, 0))
                columns.append((before - row, row, after - row))
            start = (frame * 2 + half) * 16
            for b in range(3):
                row0, row1, across = columns[0][b], columns[1][b], columns[2][b]
                above, below = across * (1.0 - upper), across * upper
                for a, value in enumerate((
                    jnp.concatenate([above - row0, row0 - row1], axis=0),
                    jnp.concatenate([row0, row1], axis=0),
                    jnp.concatenate([row1 - row0, below - row1], axis=0),
                )):
                    at = pl.ds(start, 16)
                    ops[a * 3 + b, 0, at], ops[a * 3 + b, 1, at] = split(value)
        yield
    parts = []
    for k in range(9):
        product = jnp.dot(ops[k, :, 0:rows].reshape(2 * rows, depth), space[0, k], preferred_element_type=F32)
        product = product[:rows] + product[rows:]
        parts.append(product + jnp.dot(ops[k, 0, 0:rows], space[1, k], preferred_element_type=F32))
        if k % 3 == 2:
            yield
    for up in range(2):
        base = [parts[6 * up + b] + parts[3 + b] for b in range(3)]
        for side in range(2):
            value = base[1] + base[2 * side] + space_bias[...]
            for frame in range(frames):
                for half in range(2):
                    start = (frame * 2 + half) * 16
                    for row in range(2):
                        piece = value[start + row * 8 : start + row * 8 + 8]
                        for lane in range(2):
                            stage[lane, frame * 2 + half, row * 2 + up, pl.ds(side, 8, stride=2), :] = piece[:, lane * 128 : lane * 128 + 128]
    yield
    for frame in range(frames):
        valid = (first + frame) < keep
        for half in range(2):
            for row in range(4):
                piece = jnp.concatenate([stage[lane, frame * 2 + half, row] for lane in range(2)], axis=1)
                out[(first + frame) * 2 + half, row] = jnp.where(valid, piece, 0.0)
    yield


MESH = pl.DeviceIdType.MESH
ACROSS, RIGHT, LEFT, ACROSS_RIGHT, ACROSS_LEFT = range(5)
MIRROR = (ACROSS, LEFT, RIGHT, ACROSS_LEFT, ACROSS_RIGHT)
DIAGONALS, SIDES = (ACROSS_RIGHT, ACROSS_LEFT), (RIGHT, RIGHT, LEFT, LEFT)
PIECES = ((0, 8, 16), (16, 2, 24), (18, 2, 26), (8, 1, 28), (9, 1, 29))
VERTICAL, ENDS, FACING, SIDE, OTHER = range(5)
PLACES = ((0, 8), (8, 2), (16, 8), (24, 4), (32, 8))


def wide(value, times=4):
    return jnp.concatenate([value] * times, axis=-1)


def group_sums(value):
    lane = lax.broadcasted_iota(jnp.int32, value.shape, 1)
    for step in (1, 2, 4, 8):
        ahead, behind = pltpu.roll(value, 128 - step, 1), pltpu.roll(value, step, 1)
        value = value + jnp.where(lane & step == 0, ahead, behind)
    return value


def tile_neighbours(tile):
    column, row = tile % 8, tile // 8
    right, left = (column + 1) % 8, (column + 7) % 8
    own, other = row * 8, (1 - row) * 8
    return other + column, own + right, own + left, other + right, other + left


GROUP = 3


def kernel(
    offsets, lengths, raw_features, gain_in, bias_in, time_in, time_bias_in, space_in, space_bias_in, result,
    features, gain, bias, time_raw, time_bias, space_raw, space_bias,
    near, swap_out, swap_in, core_out, core_in, halo, block,
    marks, mark_in, kinds, sums, sums_in, norms, norms_in,
    time, space, act, temporal, ops, stage, out,
    near_sem, swap_sem, core_sem, halo_sem, mark_sem, sums_sem, norms_sem, load_sem, store_sem,
):
    frames = raw_features.shape[0]
    groups = frames // GROUP
    grp, tile = lax.axis_index("grp"), lax.axis_index("tile")
    neighbours = tile_neighbours(tile)
    facing = 1 - tile // 8
    has_left, has_right = tile % 8 != 0, tile % 8 != 7

    loads = [
        pltpu.make_async_copy(source, target, load_sem.at[at])
        for at, (source, target) in enumerate((
            (raw_features.at[:, pl.ds(pl.multiple_of(facing * 8, 8), 8)], features.at[0]), (time_in, time_raw), (space_in, space_raw), (gain_in, gain),
            (bias_in, bias), (time_bias_in, time_bias), (space_bias_in, space_bias),
            (raw_features.at[:, pl.ds(pl.multiple_of(8 - facing * 8, 8), 8)], features.at[1]),
        ))
    ]
    for load in loads[7:] + loads[:7]:
        load.start()

    def send(source, target, sems, at, device):
        out_sem, in_sem = sems
        return pltpu.make_async_remote_copy(
            src_ref=source, dst_ref=target, send_sem=out_sem.at[at], recv_sem=in_sem.at[at],
            device_id=device, device_id_type=MESH,
        )

    def near_copy(step, half, group):
        start = facing * 8 if half == 0 else 8 - facing * 8
        source = raw_features.at[pl.ds(group * GROUP, GROUP), pl.ds(pl.multiple_of(start, 8), 8)]
        return send(source, near.at[step - 1, half, pl.ds(group * GROUP, GROUP)], near_sem, (step - 1, half, group), (grp ^ (step * 2), tile))

    def swap_copy(part, group):
        rows = pl.ds(*PLACES[part])
        at = pl.ds(group * GROUP, GROUP)
        return send(swap_out.at[at, rows], swap_in.at[at, rows], swap_sem, (part, group), (grp ^ 8, tile))

    def core_copy(part, group):
        rows = pl.ds(*PLACES[part])
        at = pl.ds(group * GROUP, GROUP)
        return send(core_out.at[at, rows], core_in.at[at, rows], core_sem, (part, group), (grp ^ 1, tile))

    def halo_copy(kind, group):
        start, count, land = PIECES[kind]
        at = pl.ds(group * GROUP, GROUP)
        return send(
            halo.at[at, pl.ds(start, count)], block.at[at, pl.ds(land, count)],
            halo_sem, (kind, group), (grp, neighbours[kind]),
        )

    def where_there(kind, there_right, there_left, action):
        if kind == ACROSS:
            action()
        else:
            pl.when(there_right if kind in (RIGHT, ACROSS_RIGHT) else there_left)(action)

    def start_piece(kind, group):
        where_there(kind, has_right, has_left, lambda: halo_copy(kind, group).start())

    def piece_sent(kind, group):
        where_there(kind, has_right, has_left, lambda: halo_copy(kind, group).wait_send())

    def piece_landed(kind, group):
        where_there(kind, has_left, has_right, lambda: halo_copy(kind, group).wait_recv())

    def mark_copy(kind):
        return send(marks, mark_in.at[MIRROR[kind]], mark_sem, MIRROR[kind], (grp, neighbours[kind]))

    def sums_copy(step):
        return send(sums, sums_in.at[step], sums_sem, step, (grp, (tile + step) % 16))

    def norms_copy(step):
        return send(norms, norms_in.at[step], norms_sem, step, (grp ^ step, tile))

    barrier = pltpu.get_barrier_semaphore()

    @pl.loop(1, 16)
    def _(step):
        pl.semaphore_signal(barrier, inc=1, device_id=(grp, (tile + step) % 16), device_id_type=MESH)
        pl.semaphore_signal(barrier, inc=1, device_id=(grp ^ step, tile), device_id_type=MESH)

    marks[...] = jnp.full(marks.shape, offsets[0], jnp.int32)
    act[:, 0:2] = jnp.zeros((2, 2, 32, 512), BF16)
    pl.semaphore_wait(barrier, 30)
    for kind in range(5):
        mark_copy(kind).start()

    def start_near(half):
        for group in range(groups):
            for step in (1, 2, 3):
                near_copy(step, half, group).start()

    start_near(0)

    length = lengths[grp]
    loads[0].wait()
    loads[7].wait()
    total, squares = jnp.zeros((8, 512), F32), jnp.zeros((8, 512), F32)
    for frame in range(frames):
        for row in range(2):
            value = jnp.where(frame < length, features[row, frame], 0.0)
            total, squares = total + value, squares + value * value
    total, squares = jnp.sum(total, axis=0, keepdims=True), jnp.sum(squares, axis=0, keepdims=True)
    for part in range(4):
        sums[part : part + 1] = total[:, part * 128 : part * 128 + 128]
        sums[part + 4 : part + 5] = squares[:, part * 128 : part * 128 + 128]

    @pl.loop(1, 16)
    def _(step):
        sums_copy(step).start()

    start_near(1)

    kinds[0] = marks[...]

    def chosen(half, rows, frame, mark):
        pick = wide(mark // 2 % 4)
        value = features[half, frame, rows]
        for step in (1, 2, 3):
            value = jnp.where(pick == step, near[step - 1, half, frame, rows], value)
        return value

    def learn_marks():
        for kind in range(5):
            mark_copy(kind).wait_recv()
        kinds[1] = mark_in[ACROSS]
        for at, picked in ((2, DIAGONALS), (3, SIDES)):
            kinds[at] = jnp.concatenate([mark_in[kind][0:1] for kind in picked] + [marks[len(picked) :]], axis=0)

    def wait_near(half, group):
        for step in (1, 2, 3):
            near_copy(step, half, group).wait_recv()

    def members(group):
        return range(group * GROUP, group * GROUP + GROUP)

    def swap_part(part, group):
        start, count = PLACES[part]
        rows = pl.ds(0, 8)
        for frame in members(group):
            if part == VERTICAL:
                swap_out[frame, start : start + 8] = chosen(0, rows, frame, kinds[1])
            elif part in (FACING, OTHER):
                swap_out[frame, start : start + 8] = chosen(int(part == OTHER), rows, frame, kinds[0])
            else:
                cells = ((0, 7), (0, 0)) if part == ENDS else ((0, 7), (1, 7), (0, 0), (1, 0))
                for place, (half, cell) in enumerate(cells):
                    mark = kinds[2 if part == ENDS else 3, place : place + 1]
                    swap_out[frame, start + place : start + place + 1] = chosen(half, pl.ds(cell, 1), frame, mark)
        swap_copy(part, group).start()

    def mark_of(part):
        return wide(kinds[(1, 2, 0, 3, 0)[part]])

    def core_part(part, group):
        swap_copy(part, group).wait_recv()
        rows = slice(PLACES[part][0], PLACES[part][0] + 8)
        crossed = mark_of(part) // 8 == 1
        for frame in members(group):
            core_out[frame, rows] = jnp.where(crossed, swap_in[frame, rows], swap_out[frame, rows])
        core_copy(part, group).start()

    def finals(part, group, target, at):
        core_copy(part, group).wait_recv()
        rows = slice(PLACES[part][0], PLACES[part][0] + 8)
        crossed = mark_of(part) % 2 == 1
        for frame in members(group):
            target[frame, at : at + 8] = jnp.where(crossed, core_in[frame, rows], core_out[frame, rows])

    def send_vertical(group):
        for part, kinds_sent in ((VERTICAL, (ACROSS,)), (ENDS, DIAGONALS)):
            finals(part, group, halo, part * 8)
            for kind in kinds_sent:
                start_piece(kind, group)

    def send_sides(group):
        finals(SIDE, group, halo, 16)
        for kind in (RIGHT, LEFT):
            start_piece(kind, group)

    def finish(group):
        finals(FACING, group, block, 0)
        finals(OTHER, group, block, 8)

    def start_norms():
        @pl.loop(1, 16)
        def _(other):
            sums_copy(other).wait_recv()

        value = sums[...]
        for other in range(1, 16):
            value = value + sums_in[other]
        value = group_sums(value) / (length.astype(F32) * 4096.0)
        mean = value[0:4]
        norms[0:4] = mean
        norms[4:8] = 1.0 / jnp.sqrt(value[4:8] - mean * mean + 1e-6)

        @pl.loop(1, 16)
        def _(other):
            norms_copy(other).start()

    def swap_vertical(group):
        swap_part(VERTICAL, group)
        swap_part(ENDS, group)

    def core_vertical(group):
        core_part(VERTICAL, group)
        core_part(ENDS, group)

    def swap_other(group):
        swap_part(SIDE, group)
        swap_part(OTHER, group)

    def core_other(group):
        core_part(SIDE, group)
        core_part(OTHER, group)

    wait_near(0, 0)
    swap_part(FACING, 0)
    loads[1].wait()

    @pl.loop(0, 24)
    def _(piece):
        prepare_time(piece, time_raw, time)

    learn_marks()
    swap_vertical(0)
    wait_near(0, 1)
    swap_vertical(1)
    swap_part(FACING, 1)
    loads[2].wait()

    @pl.loop(0, 16)
    def _(piece):
        prepare_space(piece, space_raw, space)

    wait_near(0, 2)
    swap_vertical(2)
    swap_part(FACING, 2)
    start_norms()
    core_vertical(0)
    wait_near(1, 0)
    swap_other(0)
    core_vertical(1)
    send_vertical(0)
    core_part(FACING, 0)
    wait_near(1, 1)
    swap_other(1)
    core_vertical(2)
    send_vertical(1)
    core_part(FACING, 1)
    core_other(0)
    wait_near(1, 2)
    swap_other(2)
    send_vertical(2)
    send_sides(0)
    core_part(FACING, 2)
    finish(0)

    @pl.loop(1, 16)
    def _(other):
        norms_copy(other).wait_recv()

    for load in loads[3:7]:
        load.wait()
    value = norms[...]
    for other in range(1, 16):
        value = jnp.where(marks[...] == other, norms_in[other], value)
    mean, scale = (
        jnp.concatenate([value[row + i : row + i + 1] for i in range(4)], axis=1) for row in (0, 4)
    )
    number = lambda flag: flag.astype(F32)
    upper = number(tile < 8)
    keep = lengths[grp ^ offsets[0]]

    def store(first, count):
        rows = pl.ds(first * 2, count * 2)
        return pltpu.make_async_copy(out.at[rows], result.at[rows], store_sem.at[first])

    def compute():
        first = 0
        for count in [GROUP] * groups:
            for kind in range(5):
                piece_landed(kind, first // GROUP)
            normalize(first, count, block, mean, scale, gain[...], bias[...], act)
            yield
            yield from decode(
                first, count, keep, facing, upper, has_left, has_right, act, time, time_bias, space, space_bias,
                temporal, ops, stage, out,
            )
            store(first, count).start()
            first += count

    def transfers():
        core_other(1)
        yield
        send_sides(1)
        yield
        yield
        core_other(2)
        yield
        finish(1)
        yield
        send_sides(2)
        finish(2)

    work, moves = compute(), transfers()
    for _ in moves:
        next(work)
    for _ in work:
        pass

    first = 0
    for count in [GROUP] * groups:
        store(first, count).wait()
        first += count
    for kind in range(5):
        mark_copy(kind).wait_send()

    @pl.loop(1, 16)
    def _(other):
        sums_copy(other).wait_send()
        norms_copy(other).wait_send()

    for group in range(groups):
        for half in range(2):
            for step in (1, 2, 3):
                near_copy(step, half, group).wait_send()
        for part in range(5):
            swap_copy(part, group).wait_send()
            core_copy(part, group).wait_send()
        for kind in range(5):
            piece_sent(kind, group)


def decoded(offsets, lengths, features, gain, bias, time_weight, time_bias, space_weight, space_bias):
    frames = features.shape[0]
    scalars, anywhere = pl.BlockSpec(memory_space=pltpu.SMEM), pl.BlockSpec(memory_space=pl.ANY)
    sems = lambda *shape: [[pltpu.SemaphoreType.DMA(shape)] * 2]
    buffer = lambda *shape, kind=F32: pltpu.VMEM(shape, kind)
    most = GROUP
    arrays = (features, gain, bias, time_weight, time_bias, space_weight, space_bias)
    return pl.pallas_call(
        kernel,
        out_shape=jax.ShapeDtypeStruct((2 * frames, 4, 16, 256), F32),
        in_specs=[scalars, scalars] + [anywhere] * 7,
        out_specs=anywhere,
        scratch_shapes=[buffer(2, frames, 8, 512)] + [buffer(*array.shape) for array in arrays[1:]]
        + [buffer(3, 2, frames, 8, 512)]
        + [buffer(frames, 40, 512)] * 4
        + [buffer(frames, 24, 512), buffer(frames, 32, 512)]
        + [buffer(*shape, kind=jnp.int32) for shape in ((8, 128), (5, 8, 128), (4, 8, 128))]
        + [buffer(8, 128), buffer(16, 8, 128)] * 2
        + [buffer(2, *time_weight.shape, kind=BF16), buffer(2, 9, 512, 256, kind=BF16)]
        + [buffer(2, frames + 2, 32, 512, kind=BF16), buffer(most * 32, 1024), buffer(9, 2, most * 32, 512, kind=BF16)]
        + [buffer(2, most * 2, 4, 16, 128), buffer(2 * frames, 4, 16, 256)]
        + sems(3, 2, frames // GROUP) + sems(5, frames // GROUP) * 3 + sems(5) + sems(16) * 2
        + [pltpu.SemaphoreType.DMA((len(arrays) + 1,)), pltpu.SemaphoreType.DMA((frames,))],
        compiler_params=pltpu.CompilerParams(
            collective_id=0, has_side_effects=True, vmem_limit_bytes=58 * 2**20
        ),
    )(offsets, lengths, *arrays)


def on_device(features, lengths, offsets, norm_gain, norm_bias, time_weight, time_bias, space_weight, space_bias):
    frames, channels = features.shape[2], features.shape[-1]
    row = lambda array: array.reshape(1, -1)
    result = decoded(
        offsets, lengths, features.reshape(frames, 16, channels), row(norm_gain), row(norm_bias),
        time_weight, row(time_bias), space_weight, row(space_bias),
    )
    return result[None, None]


def solution(mesh):
    in_specs = (P("grp", "tile", None, None, None, None), P(), P("tile"), P(), P(), P(), P(), P(), P())
    out_specs = P("grp", "tile", None, None, None, None)
    return jax.shard_map(on_device, mesh=mesh, in_specs=in_specs, out_specs=out_specs, check_vma=False)
```

```python
import jax
import jax.numpy as jnp
from jax import lax
from jax.experimental import pallas as pl
from jax.experimental.pallas import tpu as pltpu
from jax.sharding import PartitionSpec as P

F32, BF16 = jnp.float32, jnp.bfloat16


def split(value):
    high = value.astype(BF16)
    return high, (value - high.astype(F32)).astype(BF16)


def prepare_time(step, raw, both):
    rows = 64
    depth = raw.shape[1]
    tap = step // (depth // rows)
    at = pl.ds(pl.multiple_of(step % (depth // rows) * rows, rows), rows)
    both[0, tap, at], both[1, tap, at] = split(raw[tap, at])


def prepare_space(step, raw, both):
    rows = 32
    at = pl.ds(pl.multiple_of(step * rows, rows), rows)
    kernel = [[raw[a, b, at] for b in range(3)] for a in range(3)]
    by_row = [kernel[0], [kernel[0][b] + kernel[1][b] + kernel[2][b] for b in range(3)], kernel[2]]
    for a in range(3):
        one = by_row[a]
        for b, value in enumerate((one[0], one[0] + one[1] + one[2], one[2])):
            both[0, a * 3 + b, at], both[1, a * 3 + b, at] = split(value)


def normalize(first, count, block, mean, scale, gain, bias, act):
    for frame in range(first, first + count):
        inner = (block[frame] - mean) * scale * gain + bias
        inner = inner / (1.0 + jnp.exp(-inner))
        act[0, frame + 2], act[1, frame + 2] = split(inner)


def decode(first, frames, keep, facing, upper, has_left, has_right, act, time, time_bias, space, space_bias, temporal, ops, stage, out):
    rows, depth = frames * 32, act.shape[-1]
    both, high = [], []
    for tap in range(3):
        at = pl.ds(first + tap, frames)
        both.append(act[:, at].reshape(2 * rows, depth))
        high.append(act[0, at].reshape(rows, depth))
    weights = time.reshape(2, 3 * depth, 2 * depth)
    product = jnp.dot(jnp.concatenate(both, axis=1), weights[0], preferred_element_type=F32)
    yield
    rest = jnp.dot(jnp.concatenate(high, axis=1), weights[1], preferred_element_type=F32)
    temporal[0:rows] = product[:rows] + product[rows:] + rest + time_bias[...]
    yield
    place = lax.broadcasted_iota(jnp.int32, (8, depth), 0)
    for frame in range(frames):
        for half in range(2):
            lanes = slice(half * depth, half * depth + depth)
            block = lambda i: temporal[pl.ds(pl.multiple_of(frame * 32 + i * 8, 8), 8), lanes]
            side = lambda i: temporal[pl.ds(frame * 32 + 24 + i, 1), lanes]
            other = 1 - facing
            columns = []
            for row, left, right in (
                (block(facing), facing, 2 + facing), (block(other), other, 2 + other), (block(2), 4, 5),
            ):
                before = jnp.where(place == 0, jnp.where(has_left, side(left), 0.0), pltpu.roll(row, 1, 0))
                after = jnp.where(place == 7, jnp.where(has_right, side(right), 0.0), pltpu.roll(row, 7, 0))
                columns.append((before - row, row, after - row))
            start = (frame * 2 + half) * 16
            for b in range(3):
                row0, row1, across = columns[0][b], columns[1][b], columns[2][b]
                above, below = across * (1.0 - upper), across * upper
                for a, value in enumerate((
                    jnp.concatenate([above - row0, row0 - row1], axis=0),
                    jnp.concatenate([row0, row1], axis=0),
                    jnp.concatenate([row1 - row0, below - row1], axis=0),
                )):
                    at = pl.ds(start, 16)
                    ops[a * 3 + b, 0, at], ops[a * 3 + b, 1, at] = split(value)
        yield
    parts = []
    for k in range(9):
        product = jnp.dot(ops[k, :, 0:rows].reshape(2 * rows, depth), space[0, k], preferred_element_type=F32)
        product = product[:rows] + product[rows:]
        parts.append(product + jnp.dot(ops[k, 0, 0:rows], space[1, k], preferred_element_type=F32))
        if k % 3 == 2:
            yield
    for up in range(2):
        base = [parts[6 * up + b] + parts[3 + b] for b in range(3)]
        for side in range(2):
            value = base[1] + base[2 * side] + space_bias[...]
            for frame in range(frames):
                for half in range(2):
                    start = (frame * 2 + half) * 16
                    for row in range(2):
                        piece = value[start + row * 8 : start + row * 8 + 8]
                        for lane in range(2):
                            stage[lane, frame * 2 + half, row * 2 + up, pl.ds(side, 8, stride=2), :] = piece[:, lane * 128 : lane * 128 + 128]
    yield
    for frame in range(frames):
        valid = (first + frame) < keep
        for half in range(2):
            for row in range(4):
                piece = jnp.concatenate([stage[lane, frame * 2 + half, row] for lane in range(2)], axis=1)
                out[(first + frame) * 2 + half, row] = jnp.where(valid, piece, 0.0)
    yield


MESH = pl.DeviceIdType.MESH
ACROSS, RIGHT, LEFT, ACROSS_RIGHT, ACROSS_LEFT = range(5)
MIRROR = (ACROSS, LEFT, RIGHT, ACROSS_LEFT, ACROSS_RIGHT)
DIAGONALS, SIDES = (ACROSS_RIGHT, ACROSS_LEFT), (RIGHT, RIGHT, LEFT, LEFT)
PIECES = ((0, 8, 16), (16, 2, 24), (18, 2, 26), (8, 1, 28), (9, 1, 29))
VERTICAL, ENDS, FACING, SIDE, OTHER = range(5)
PLACES = ((0, 8), (8, 2), (16, 8), (24, 4), (32, 8))


def wide(value, times=4):
    return jnp.concatenate([value] * times, axis=-1)


def group_sums(value):
    lane = lax.broadcasted_iota(jnp.int32, value.shape, 1)
    for step in (1, 2, 4, 8):
        ahead, behind = pltpu.roll(value, 128 - step, 1), pltpu.roll(value, step, 1)
        value = value + jnp.where(lane & step == 0, ahead, behind)
    return value


def tile_neighbours(tile):
    column, row = tile % 8, tile // 8
    right, left = (column + 1) % 8, (column + 7) % 8
    own, other = row * 8, (1 - row) * 8
    return other + column, own + right, own + left, other + right, other + left


GROUP = 3


def kernel(
    offsets, lengths, raw_features, gain_in, bias_in, time_in, time_bias_in, space_in, space_bias_in, result,
    features, gain, bias, time_raw, time_bias, space_raw, space_bias,
    near, swap_out, swap_in, core_out, core_in, halo, block,
    marks, mark_in, kinds, sums, sums_in, norms, norms_in,
    time, space, act, temporal, ops, stage, out,
    near_sem, swap_sem, core_sem, halo_sem, mark_sem, sums_sem, norms_sem, load_sem, store_sem,
):
    frames = raw_features.shape[0]
    groups = frames // GROUP
    grp, tile = lax.axis_index("grp"), lax.axis_index("tile")
    neighbours = tile_neighbours(tile)
    facing = 1 - tile // 8
    has_left, has_right = tile % 8 != 0, tile % 8 != 7

    loads = [
        pltpu.make_async_copy(source, target, load_sem.at[at])
        for at, (source, target) in enumerate((
            (raw_features.at[:, pl.ds(pl.multiple_of(facing * 8, 8), 8)], features.at[0]), (time_in, time_raw), (space_in, space_raw), (gain_in, gain),
            (bias_in, bias), (time_bias_in, time_bias), (space_bias_in, space_bias),
            (raw_features.at[:, pl.ds(pl.multiple_of(8 - facing * 8, 8), 8)], features.at[1]),
        ))
    ]
    for load in loads[7:] + loads[:7]:
        load.start()

    def send(source, target, sems, at, device):
        out_sem, in_sem = sems
        return pltpu.make_async_remote_copy(
            src_ref=source, dst_ref=target, send_sem=out_sem.at[at], recv_sem=in_sem.at[at],
            device_id=device, device_id_type=MESH,
        )

    def near_copy(step, half, group):
        start = facing * 8 if half == 0 else 8 - facing * 8
        source = raw_features.at[pl.ds(group * GROUP, GROUP), pl.ds(pl.multiple_of(start, 8), 8)]
        return send(source, near.at[step - 1, half, pl.ds(group * GROUP, GROUP)], near_sem, (step - 1, half, group), (grp ^ (step * 2), tile))

    def swap_copy(part, group):
        rows = pl.ds(*PLACES[part])
        at = pl.ds(group * GROUP, GROUP)
        return send(swap_out.at[at, rows], swap_in.at[at, rows], swap_sem, (part, group), (grp ^ 8, tile))

    def core_copy(part, group):
        rows = pl.ds(*PLACES[part])
        at = pl.ds(group * GROUP, GROUP)
        return send(core_out.at[at, rows], core_in.at[at, rows], core_sem, (part, group), (grp ^ 1, tile))

    def halo_copy(kind, group):
        start, count, land = PIECES[kind]
        at = pl.ds(group * GROUP, GROUP)
        return send(
            halo.at[at, pl.ds(start, count)], block.at[at, pl.ds(land, count)],
            halo_sem, (kind, group), (grp, neighbours[kind]),
        )

    def where_there(kind, there_right, there_left, action):
        if kind == ACROSS:
            action()
        else:
            pl.when(there_right if kind in (RIGHT, ACROSS_RIGHT) else there_left)(action)

    def start_piece(kind, group):
        where_there(kind, has_right, has_left, lambda: halo_copy(kind, group).start())

    def piece_sent(kind, group):
        where_there(kind, has_right, has_left, lambda: halo_copy(kind, group).wait_send())

    def piece_landed(kind, group):
        where_there(kind, has_left, has_right, lambda: halo_copy(kind, group).wait_recv())

    def mark_copy(kind):
        return send(marks, mark_in.at[MIRROR[kind]], mark_sem, MIRROR[kind], (grp, neighbours[kind]))

    def sums_copy(step):
        return send(sums, sums_in.at[step], sums_sem, step, (grp, (tile + step) % 16))

    def norms_copy(step):
        return send(norms, norms_in.at[step], norms_sem, step, (grp ^ step, tile))

    barrier = pltpu.get_barrier_semaphore()

    @pl.loop(1, 16)
    def _(step):
        pl.semaphore_signal(barrier, inc=1, device_id=(grp, (tile + step) % 16), device_id_type=MESH)
        pl.semaphore_signal(barrier, inc=1, device_id=(grp ^ step, tile), device_id_type=MESH)

    marks[...] = jnp.full(marks.shape, offsets[0], jnp.int32)
    act[:, 0:2] = jnp.zeros((2, 2, 32, 512), BF16)
    pl.semaphore_wait(barrier, 30)
    for kind in range(5):
        mark_copy(kind).start()

    def start_near(half, group):
        for step in (1, 2, 3):
            near_copy(step, half, group).start()

    start_near(0, 0)
    start_near(0, 1)

    length = lengths[grp]
    loads[0].wait()
    loads[7].wait()
    total, squares = jnp.zeros((8, 512), F32), jnp.zeros((8, 512), F32)
    for frame in range(frames):
        for row in range(2):
            value = jnp.where(frame < length, features[row, frame], 0.0)
            total, squares = total + value, squares + value * value
    total, squares = jnp.sum(total, axis=0, keepdims=True), jnp.sum(squares, axis=0, keepdims=True)
    for part in range(4):
        sums[part : part + 1] = total[:, part * 128 : part * 128 + 128]
        sums[part + 4 : part + 5] = squares[:, part * 128 : part * 128 + 128]

    @pl.loop(1, 16)
    def _(step):
        sums_copy(step).start()

    for half, group in ((1, 0), (0, 2), (1, 1), (1, 2)):
        start_near(half, group)

    kinds[0] = marks[...]

    def chosen(half, rows, frame, mark):
        pick = wide(mark // 2 % 4)
        value = features[half, frame, rows]
        for step in (1, 2, 3):
            value = jnp.where(pick == step, near[step - 1, half, frame, rows], value)
        return value

    def learn_marks():
        for kind in range(5):
            mark_copy(kind).wait_recv()
        kinds[1] = mark_in[ACROSS]
        for at, picked in ((2, DIAGONALS), (3, SIDES)):
            kinds[at] = jnp.concatenate([mark_in[kind][0:1] for kind in picked] + [marks[len(picked) :]], axis=0)

    def wait_near(half, group):
        for step in (1, 2, 3):
            near_copy(step, half, group).wait_recv()

    def members(group):
        return range(group * GROUP, group * GROUP + GROUP)

    def swap_part(part, group):
        start, count = PLACES[part]
        rows = pl.ds(0, 8)
        for frame in members(group):
            if part == VERTICAL:
                swap_out[frame, start : start + 8] = chosen(0, rows, frame, kinds[1])
            elif part in (FACING, OTHER):
                swap_out[frame, start : start + 8] = chosen(int(part == OTHER), rows, frame, kinds[0])
            else:
                cells = ((0, 7), (0, 0)) if part == ENDS else ((0, 7), (1, 7), (0, 0), (1, 0))
                for place, (half, cell) in enumerate(cells):
                    mark = kinds[2 if part == ENDS else 3, place : place + 1]
                    swap_out[frame, start + place : start + place + 1] = chosen(half, pl.ds(cell, 1), frame, mark)
        swap_copy(part, group).start()

    def mark_of(part):
        return wide(kinds[(1, 2, 0, 3, 0)[part]])

    def core_part(part, group):
        swap_copy(part, group).wait_recv()
        rows = slice(PLACES[part][0], PLACES[part][0] + 8)
        crossed = mark_of(part) // 8 == 1
        for frame in members(group):
            core_out[frame, rows] = jnp.where(crossed, swap_in[frame, rows], swap_out[frame, rows])
        core_copy(part, group).start()

    def finals(part, group, target, at):
        core_copy(part, group).wait_recv()
        rows = slice(PLACES[part][0], PLACES[part][0] + 8)
        crossed = mark_of(part) % 2 == 1
        for frame in members(group):
            target[frame, at : at + 8] = jnp.where(crossed, core_in[frame, rows], core_out[frame, rows])

    def send_vertical(group):
        for part, kinds_sent in ((VERTICAL, (ACROSS,)), (ENDS, DIAGONALS)):
            finals(part, group, halo, part * 8)
            for kind in kinds_sent:
                start_piece(kind, group)

    def send_sides(group):
        finals(SIDE, group, halo, 16)
        for kind in (RIGHT, LEFT):
            start_piece(kind, group)

    def finish(group):
        finals(FACING, group, block, 0)
        finals(OTHER, group, block, 8)

    def start_norms():
        @pl.loop(1, 16)
        def _(other):
            sums_copy(other).wait_recv()

        value = sums[...]
        for other in range(1, 16):
            value = value + sums_in[other]
        value = group_sums(value) / (length.astype(F32) * 4096.0)
        mean = value[0:4]
        norms[0:4] = mean
        norms[4:8] = 1.0 / jnp.sqrt(value[4:8] - mean * mean + 1e-6)

        @pl.loop(1, 16)
        def _(other):
            norms_copy(other).start()

    def swap_vertical(group):
        swap_part(VERTICAL, group)
        swap_part(ENDS, group)

    def core_vertical(group):
        core_part(VERTICAL, group)
        core_part(ENDS, group)

    def swap_other(group):
        swap_part(SIDE, group)
        swap_part(OTHER, group)

    def core_other(group):
        core_part(SIDE, group)
        core_part(OTHER, group)

    wait_near(0, 0)
    swap_part(FACING, 0)
    loads[1].wait()

    @pl.loop(0, 24)
    def _(piece):
        prepare_time(piece, time_raw, time)

    learn_marks()
    swap_vertical(0)
    wait_near(0, 1)
    swap_vertical(1)
    loads[2].wait()

    @pl.loop(0, 16)
    def _(piece):
        prepare_space(piece, space_raw, space)

    wait_near(1, 0)
    swap_other(0)
    swap_part(FACING, 1)
    start_norms()
    core_vertical(0)
    wait_near(0, 2)
    swap_vertical(2)
    core_vertical(1)
    send_vertical(0)
    core_part(FACING, 0)
    wait_near(1, 1)
    swap_other(1)
    swap_part(FACING, 2)
    core_other(0)
    send_vertical(1)
    core_part(FACING, 1)
    send_sides(0)
    wait_near(1, 2)
    swap_other(2)
    core_vertical(2)
    finish(0)
    send_vertical(2)
    core_part(FACING, 2)

    @pl.loop(1, 16)
    def _(other):
        norms_copy(other).wait_recv()

    for load in loads[3:7]:
        load.wait()
    value = norms[...]
    for other in range(1, 16):
        value = jnp.where(marks[...] == other, norms_in[other], value)
    mean, scale = (
        jnp.concatenate([value[row + i : row + i + 1] for i in range(4)], axis=1) for row in (0, 4)
    )
    number = lambda flag: flag.astype(F32)
    upper = number(tile < 8)
    keep = lengths[grp ^ offsets[0]]

    def store(first, count):
        rows = pl.ds(first * 2, count * 2)
        return pltpu.make_async_copy(out.at[rows], result.at[rows], store_sem.at[first])

    def compute():
        first = 0
        for count in [GROUP] * groups:
            for kind in range(5):
                piece_landed(kind, first // GROUP)
            normalize(first, count, block, mean, scale, gain[...], bias[...], act)
            yield
            yield from decode(
                first, count, keep, facing, upper, has_left, has_right, act, time, time_bias, space, space_bias,
                temporal, ops, stage, out,
            )
            store(first, count).start()
            first += count

    def transfers():
        core_other(1)
        yield
        send_sides(1)
        yield
        yield
        core_other(2)
        yield
        finish(1)
        yield
        send_sides(2)
        finish(2)

    work, moves = compute(), transfers()
    for _ in moves:
        next(work)
    for _ in work:
        pass

    first = 0
    for count in [GROUP] * groups:
        store(first, count).wait()
        first += count
    for kind in range(5):
        mark_copy(kind).wait_send()

    @pl.loop(1, 16)
    def _(other):
        sums_copy(other).wait_send()
        norms_copy(other).wait_send()

    for group in range(groups):
        for half in range(2):
            for step in (1, 2, 3):
                near_copy(step, half, group).wait_send()
        for part in range(5):
            swap_copy(part, group).wait_send()
            core_copy(part, group).wait_send()
        for kind in range(5):
            piece_sent(kind, group)


def decoded(offsets, lengths, features, gain, bias, time_weight, time_bias, space_weight, space_bias):
    frames = features.shape[0]
    scalars, anywhere = pl.BlockSpec(memory_space=pltpu.SMEM), pl.BlockSpec(memory_space=pl.ANY)
    sems = lambda *shape: [[pltpu.SemaphoreType.DMA(shape)] * 2]
    buffer = lambda *shape, kind=F32: pltpu.VMEM(shape, kind)
    most = GROUP
    arrays = (features, gain, bias, time_weight, time_bias, space_weight, space_bias)
    return pl.pallas_call(
        kernel,
        out_shape=jax.ShapeDtypeStruct((2 * frames, 4, 16, 256), F32),
        in_specs=[scalars, scalars] + [anywhere] * 7,
        out_specs=anywhere,
        scratch_shapes=[buffer(2, frames, 8, 512)] + [buffer(*array.shape) for array in arrays[1:]]
        + [buffer(3, 2, frames, 8, 512)]
        + [buffer(frames, 40, 512)] * 4
        + [buffer(frames, 24, 512), buffer(frames, 32, 512)]
        + [buffer(*shape, kind=jnp.int32) for shape in ((8, 128), (5, 8, 128), (4, 8, 128))]
        + [buffer(8, 128), buffer(16, 8, 128)] * 2
        + [buffer(2, *time_weight.shape, kind=BF16), buffer(2, 9, 512, 256, kind=BF16)]
        + [buffer(2, frames + 2, 32, 512, kind=BF16), buffer(most * 32, 1024), buffer(9, 2, most * 32, 512, kind=BF16)]
        + [buffer(2, most * 2, 4, 16, 128), buffer(2 * frames, 4, 16, 256)]
        + sems(3, 2, frames // GROUP) + sems(5, frames // GROUP) * 3 + sems(5) + sems(16) * 2
        + [pltpu.SemaphoreType.DMA((len(arrays) + 1,)), pltpu.SemaphoreType.DMA((frames,))],
        compiler_params=pltpu.CompilerParams(
            collective_id=0, has_side_effects=True, vmem_limit_bytes=58 * 2**20
        ),
    )(offsets, lengths, *arrays)


def on_device(features, lengths, offsets, norm_gain, norm_bias, time_weight, time_bias, space_weight, space_bias):
    frames, channels = features.shape[2], features.shape[-1]
    row = lambda array: array.reshape(1, -1)
    result = decoded(
        offsets, lengths, features.reshape(frames, 16, channels), row(norm_gain), row(norm_bias),
        time_weight, row(time_bias), space_weight, row(space_bias),
    )
    return result[None, None]


def solution(mesh):
    in_specs = (P("grp", "tile", None, None, None, None), P(), P("tile"), P(), P(), P(), P(), P(), P())
    out_specs = P("grp", "tile", None, None, None, None)
    return jax.shard_map(on_device, mesh=mesh, in_specs=in_specs, out_specs=out_specs, check_vma=False)
```

```python
import jax
import jax.numpy as jnp
from jax import lax
from jax.experimental import pallas as pl
from jax.experimental.pallas import tpu as pltpu
from jax.sharding import PartitionSpec as P

F32, BF16 = jnp.float32, jnp.bfloat16


def split(value):
    high = value.astype(BF16)
    return high, (value - high.astype(F32)).astype(BF16)


def prepare_time(step, raw, both):
    rows = 64
    depth = raw.shape[1]
    tap = step // (depth // rows)
    at = pl.ds(pl.multiple_of(step % (depth // rows) * rows, rows), rows)
    both[0, tap, at], both[1, tap, at] = split(raw[tap, at])


def prepare_space(step, raw, both):
    rows = 32
    at = pl.ds(pl.multiple_of(step * rows, rows), rows)
    kernel = [[raw[a, b, at] for b in range(3)] for a in range(3)]
    by_row = [kernel[0], [kernel[0][b] + kernel[1][b] + kernel[2][b] for b in range(3)], kernel[2]]
    for a in range(3):
        one = by_row[a]
        for b, value in enumerate((one[0], one[0] + one[1] + one[2], one[2])):
            both[0, a * 3 + b, at], both[1, a * 3 + b, at] = split(value)


def normalize(first, count, block, mean, scale, gain, bias, act):
    for frame in range(first, first + count):
        inner = (block[frame] - mean) * scale * gain + bias
        inner = inner / (1.0 + jnp.exp(-inner))
        act[0, frame + 2], act[1, frame + 2] = split(inner)


def decode(first, frames, keep, facing, upper, has_left, has_right, act, time, time_bias, space, space_bias, temporal, ops, stage, out):
    rows, depth = frames * 32, act.shape[-1]
    both, high = [], []
    for tap in range(3):
        at = pl.ds(first + tap, frames)
        both.append(act[:, at].reshape(2 * rows, depth))
        high.append(act[0, at].reshape(rows, depth))
    weights = time.reshape(2, 3 * depth, 2 * depth)
    product = jnp.dot(jnp.concatenate(both, axis=1), weights[0], preferred_element_type=F32)
    yield
    rest = jnp.dot(jnp.concatenate(high, axis=1), weights[1], preferred_element_type=F32)
    temporal[0:rows] = product[:rows] + product[rows:] + rest + time_bias[...]
    yield
    place = lax.broadcasted_iota(jnp.int32, (8, depth), 0)
    for frame in range(frames):
        for half in range(2):
            lanes = slice(half * depth, half * depth + depth)
            block = lambda i: temporal[pl.ds(pl.multiple_of(frame * 32 + i * 8, 8), 8), lanes]
            side = lambda i: temporal[pl.ds(frame * 32 + 24 + i, 1), lanes]
            other = 1 - facing
            columns = []
            for row, left, right in (
                (block(facing), facing, 2 + facing), (block(other), other, 2 + other), (block(2), 4, 5),
            ):
                before = jnp.where(place == 0, jnp.where(has_left, side(left), 0.0), pltpu.roll(row, 1, 0))
                after = jnp.where(place == 7, jnp.where(has_right, side(right), 0.0), pltpu.roll(row, 7, 0))
                columns.append((before - row, row, after - row))
            start = (frame * 2 + half) * 16
            for b in range(3):
                row0, row1, across = columns[0][b], columns[1][b], columns[2][b]
                above, below = across * (1.0 - upper), across * upper
                for a, value in enumerate((
                    jnp.concatenate([above - row0, row0 - row1], axis=0),
                    jnp.concatenate([row0, row1], axis=0),
                    jnp.concatenate([row1 - row0, below - row1], axis=0),
                )):
                    at = pl.ds(start, 16)
                    ops[a * 3 + b, 0, at], ops[a * 3 + b, 1, at] = split(value)
        yield
    parts = []
    for k in range(9):
        product = jnp.dot(ops[k, :, 0:rows].reshape(2 * rows, depth), space[0, k], preferred_element_type=F32)
        product = product[:rows] + product[rows:]
        parts.append(product + jnp.dot(ops[k, 0, 0:rows], space[1, k], preferred_element_type=F32))
        if k % 3 == 2:
            yield
    for up in range(2):
        base = [parts[6 * up + b] + parts[3 + b] for b in range(3)]
        for side in range(2):
            value = base[1] + base[2 * side] + space_bias[...]
            for frame in range(frames):
                for half in range(2):
                    start = (frame * 2 + half) * 16
                    for row in range(2):
                        piece = value[start + row * 8 : start + row * 8 + 8]
                        for lane in range(2):
                            stage[lane, frame * 2 + half, row * 2 + up, pl.ds(side, 8, stride=2), :] = piece[:, lane * 128 : lane * 128 + 128]
    yield
    for frame in range(frames):
        valid = (first + frame) < keep
        for half in range(2):
            for row in range(4):
                piece = jnp.concatenate([stage[lane, frame * 2 + half, row] for lane in range(2)], axis=1)
                out[(first + frame) * 2 + half, row] = jnp.where(valid, piece, 0.0)
    yield


MESH = pl.DeviceIdType.MESH
ACROSS, RIGHT, LEFT, ACROSS_RIGHT, ACROSS_LEFT = range(5)
MIRROR = (ACROSS, LEFT, RIGHT, ACROSS_LEFT, ACROSS_RIGHT)
DIAGONALS, SIDES = (ACROSS_RIGHT, ACROSS_LEFT), (RIGHT, RIGHT, LEFT, LEFT)
PIECES = ((0, 8, 16), (16, 2, 24), (18, 2, 26), (8, 1, 28), (9, 1, 29))
VERTICAL, ENDS, FACING, SIDE, OTHER = range(5)
PLACES = ((0, 8), (8, 2), (16, 8), (24, 4), (32, 8))


def wide(value, times=4):
    return jnp.concatenate([value] * times, axis=-1)


def group_sums(value):
    lane = lax.broadcasted_iota(jnp.int32, value.shape, 1)
    for step in (1, 2, 4, 8):
        ahead, behind = pltpu.roll(value, 128 - step, 1), pltpu.roll(value, step, 1)
        value = value + jnp.where(lane & step == 0, ahead, behind)
    return value


def tile_neighbours(tile):
    column, row = tile % 8, tile // 8
    right, left = (column + 1) % 8, (column + 7) % 8
    own, other = row * 8, (1 - row) * 8
    return other + column, own + right, own + left, other + right, other + left


GROUP = 3


def kernel(
    offsets, lengths, raw_features, gain_in, bias_in, time_in, time_bias_in, space_in, space_bias_in, result,
    features, gain, bias, time_raw, time_bias, space_raw, space_bias,
    near, swap_out, swap_in, core_out, core_in, halo, block,
    marks, mark_in, kinds, sums, sums_in, norms, norms_in,
    time, space, act, temporal, ops, stage, out,
    near_sem, swap_sem, core_sem, halo_sem, mark_sem, sums_sem, norms_sem, load_sem, store_sem,
):
    frames = raw_features.shape[0]
    groups = frames // GROUP
    grp, tile = lax.axis_index("grp"), lax.axis_index("tile")
    neighbours = tile_neighbours(tile)
    facing = 1 - tile // 8
    has_left, has_right = tile % 8 != 0, tile % 8 != 7

    loads = [
        pltpu.make_async_copy(source, target, load_sem.at[at])
        for at, (source, target) in enumerate((
            (raw_features.at[:, pl.ds(pl.multiple_of(facing * 8, 8), 8)], features.at[0]), (time_in, time_raw), (space_in, space_raw), (gain_in, gain),
            (bias_in, bias), (time_bias_in, time_bias), (space_bias_in, space_bias),
            (raw_features.at[:, pl.ds(pl.multiple_of(8 - facing * 8, 8), 8)], features.at[1]),
        ))
    ]
    for load in loads[7:] + loads[:7]:
        load.start()

    def send(source, target, sems, at, device):
        out_sem, in_sem = sems
        return pltpu.make_async_remote_copy(
            src_ref=source, dst_ref=target, send_sem=out_sem.at[at], recv_sem=in_sem.at[at],
            device_id=device, device_id_type=MESH,
        )

    def near_copy(step, half, group):
        start = facing * 8 if half == 0 else 8 - facing * 8
        source = raw_features.at[pl.ds(group * GROUP, GROUP), pl.ds(pl.multiple_of(start, 8), 8)]
        return send(source, near.at[step - 1, half, pl.ds(group * GROUP, GROUP)], near_sem, (step - 1, half, group), (grp ^ (step * 2), tile))

    def swap_copy(part, group):
        rows = pl.ds(*PLACES[part])
        at = pl.ds(group * GROUP, GROUP)
        return send(swap_out.at[at, rows], swap_in.at[at, rows], swap_sem, (part, group), (grp ^ 8, tile))

    def core_copy(part, group):
        rows = pl.ds(*PLACES[part])
        at = pl.ds(group * GROUP, GROUP)
        return send(core_out.at[at, rows], core_in.at[at, rows], core_sem, (part, group), (grp ^ 1, tile))

    def halo_copy(kind, group):
        start, count, land = PIECES[kind]
        at = pl.ds(group * GROUP, GROUP)
        return send(
            halo.at[at, pl.ds(start, count)], block.at[at, pl.ds(land, count)],
            halo_sem, (kind, group), (grp, neighbours[kind]),
        )

    def where_there(kind, there_right, there_left, action):
        if kind == ACROSS:
            action()
        else:
            pl.when(there_right if kind in (RIGHT, ACROSS_RIGHT) else there_left)(action)

    def start_piece(kind, group):
        where_there(kind, has_right, has_left, lambda: halo_copy(kind, group).start())

    def piece_sent(kind, group):
        where_there(kind, has_right, has_left, lambda: halo_copy(kind, group).wait_send())

    def piece_landed(kind, group):
        where_there(kind, has_left, has_right, lambda: halo_copy(kind, group).wait_recv())

    def mark_copy(kind):
        return send(marks, mark_in.at[MIRROR[kind]], mark_sem, MIRROR[kind], (grp, neighbours[kind]))

    def sums_copy(step):
        return send(sums, sums_in.at[step], sums_sem, step, (grp, (tile + step) % 16))

    def norms_copy(step):
        return send(norms, norms_in.at[step], norms_sem, step, (grp ^ step, tile))

    barrier = pltpu.get_barrier_semaphore()

    @pl.loop(1, 16)
    def _(step):
        pl.semaphore_signal(barrier, inc=1, device_id=(grp, (tile + step) % 16), device_id_type=MESH)
        pl.semaphore_signal(barrier, inc=1, device_id=(grp ^ step, tile), device_id_type=MESH)

    marks[...] = jnp.full(marks.shape, offsets[0], jnp.int32)
    act[:, 0:2] = jnp.zeros((2, 2, 32, 512), BF16)
    pl.semaphore_wait(barrier, 30)
    for kind in range(5):
        mark_copy(kind).start()

    def start_near(half, group):
        for step in (2, 1, 3):
            near_copy(step, half, group).start()

    start_near(0, 0)
    start_near(0, 1)

    length = lengths[grp]
    loads[0].wait()
    loads[7].wait()
    total, squares = jnp.zeros((8, 512), F32), jnp.zeros((8, 512), F32)
    for frame in range(frames):
        for row in range(2):
            value = jnp.where(frame < length, features[row, frame], 0.0)
            total, squares = total + value, squares + value * value
    total, squares = jnp.sum(total, axis=0, keepdims=True), jnp.sum(squares, axis=0, keepdims=True)
    for part in range(4):
        sums[part : part + 1] = total[:, part * 128 : part * 128 + 128]
        sums[part + 4 : part + 5] = squares[:, part * 128 : part * 128 + 128]

    @pl.loop(1, 16)
    def _(step):
        sums_copy(step).start()

    for half, group in ((1, 0), (0, 2), (1, 1), (1, 2)):
        start_near(half, group)

    kinds[0] = marks[...]

    def chosen(half, rows, frame, mark):
        pick = wide(mark // 2 % 4)
        value = features[half, frame, rows]
        for step in (1, 2, 3):
            value = jnp.where(pick == step, near[step - 1, half, frame, rows], value)
        return value

    def learn_marks():
        for kind in range(5):
            mark_copy(kind).wait_recv()
        kinds[1] = mark_in[ACROSS]
        for at, picked in ((2, DIAGONALS), (3, SIDES)):
            kinds[at] = jnp.concatenate([mark_in[kind][0:1] for kind in picked] + [marks[len(picked) :]], axis=0)

    def wait_near(half, group):
        for step in (1, 2, 3):
            near_copy(step, half, group).wait_recv()

    def members(group):
        return range(group * GROUP, group * GROUP + GROUP)

    def swap_part(part, group):
        start, count = PLACES[part]
        rows = pl.ds(0, 8)
        for frame in members(group):
            if part == VERTICAL:
                swap_out[frame, start : start + 8] = chosen(0, rows, frame, kinds[1])
            elif part in (FACING, OTHER):
                swap_out[frame, start : start + 8] = chosen(int(part == OTHER), rows, frame, kinds[0])
            else:
                cells = ((0, 7), (0, 0)) if part == ENDS else ((0, 7), (1, 7), (0, 0), (1, 0))
                for place, (half, cell) in enumerate(cells):
                    mark = kinds[2 if part == ENDS else 3, place : place + 1]
                    swap_out[frame, start + place : start + place + 1] = chosen(half, pl.ds(cell, 1), frame, mark)
        swap_copy(part, group).start()

    def mark_of(part):
        return wide(kinds[(1, 2, 0, 3, 0)[part]])

    def core_part(part, group):
        swap_copy(part, group).wait_recv()
        rows = slice(PLACES[part][0], PLACES[part][0] + 8)
        crossed = mark_of(part) // 8 == 1
        for frame in members(group):
            core_out[frame, rows] = jnp.where(crossed, swap_in[frame, rows], swap_out[frame, rows])
        core_copy(part, group).start()

    def finals(part, group, target, at):
        core_copy(part, group).wait_recv()
        rows = slice(PLACES[part][0], PLACES[part][0] + 8)
        crossed = mark_of(part) % 2 == 1
        for frame in members(group):
            target[frame, at : at + 8] = jnp.where(crossed, core_in[frame, rows], core_out[frame, rows])

    def send_vertical(group):
        for part, kinds_sent in ((VERTICAL, (ACROSS,)), (ENDS, DIAGONALS)):
            finals(part, group, halo, part * 8)
            for kind in kinds_sent:
                start_piece(kind, group)

    def send_sides(group):
        finals(SIDE, group, halo, 16)
        for kind in (RIGHT, LEFT):
            start_piece(kind, group)

    def finish(group):
        finals(FACING, group, block, 0)
        finals(OTHER, group, block, 8)

    def start_norms():
        @pl.loop(1, 16)
        def _(other):
            sums_copy(other).wait_recv()

        value = sums[...]
        for other in range(1, 16):
            value = value + sums_in[other]
        value = group_sums(value) / (length.astype(F32) * 4096.0)
        mean = value[0:4]
        norms[0:4] = mean
        norms[4:8] = 1.0 / jnp.sqrt(value[4:8] - mean * mean + 1e-6)

        @pl.loop(1, 16)
        def _(other):
            norms_copy(other).start()

    def swap_vertical(group):
        swap_part(VERTICAL, group)
        swap_part(ENDS, group)

    def core_vertical(group):
        core_part(VERTICAL, group)
        core_part(ENDS, group)

    def swap_other(group):
        swap_part(SIDE, group)
        swap_part(OTHER, group)

    def core_other(group):
        core_part(SIDE, group)
        core_part(OTHER, group)

    wait_near(0, 0)
    swap_part(FACING, 0)
    learn_marks()
    swap_vertical(0)
    wait_near(0, 1)
    swap_vertical(1)
    loads[1].wait()

    @pl.loop(0, 24)
    def _(piece):
        prepare_time(piece, time_raw, time)

    wait_near(1, 0)
    swap_other(0)
    swap_part(FACING, 1)
    start_norms()
    core_vertical(0)
    loads[2].wait()

    @pl.loop(0, 16)
    def _(piece):
        prepare_space(piece, space_raw, space)

    wait_near(0, 2)
    swap_vertical(2)
    core_vertical(1)
    send_vertical(0)
    core_part(FACING, 0)
    wait_near(1, 1)
    swap_other(1)
    swap_part(FACING, 2)
    core_other(0)
    send_vertical(1)
    core_part(FACING, 1)
    send_sides(0)
    wait_near(1, 2)
    swap_other(2)
    core_vertical(2)
    finish(0)
    send_vertical(2)
    core_part(FACING, 2)

    @pl.loop(1, 16)
    def _(other):
        norms_copy(other).wait_recv()

    for load in loads[3:7]:
        load.wait()
    value = norms[...]
    for other in range(1, 16):
        value = jnp.where(marks[...] == other, norms_in[other], value)
    mean, scale = (
        jnp.concatenate([value[row + i : row + i + 1] for i in range(4)], axis=1) for row in (0, 4)
    )
    number = lambda flag: flag.astype(F32)
    upper = number(tile < 8)
    keep = lengths[grp ^ offsets[0]]

    def store(first, count):
        rows = pl.ds(first * 2, count * 2)
        return pltpu.make_async_copy(out.at[rows], result.at[rows], store_sem.at[first])

    def compute():
        first = 0
        for count in [GROUP] * groups:
            for kind in range(5):
                piece_landed(kind, first // GROUP)
            normalize(first, count, block, mean, scale, gain[...], bias[...], act)
            yield
            yield from decode(
                first, count, keep, facing, upper, has_left, has_right, act, time, time_bias, space, space_bias,
                temporal, ops, stage, out,
            )
            store(first, count).start()
            first += count

    def transfers():
        core_other(1)
        yield
        send_sides(1)
        yield
        core_other(2)
        yield
        send_sides(2)
        finish(1)
        yield
        finish(2)

    work, moves = compute(), transfers()
    for _ in moves:
        next(work)
    for _ in work:
        pass

    first = 0
    for count in [GROUP] * groups:
        store(first, count).wait()
        first += count
    for kind in range(5):
        mark_copy(kind).wait_send()

    @pl.loop(1, 16)
    def _(other):
        sums_copy(other).wait_send()
        norms_copy(other).wait_send()

    for group in range(groups):
        for half in range(2):
            for step in (1, 2, 3):
                near_copy(step, half, group).wait_send()
        for part in range(5):
            swap_copy(part, group).wait_send()
            core_copy(part, group).wait_send()
        for kind in range(5):
            piece_sent(kind, group)


def decoded(offsets, lengths, features, gain, bias, time_weight, time_bias, space_weight, space_bias):
    frames = features.shape[0]
    scalars, anywhere = pl.BlockSpec(memory_space=pltpu.SMEM), pl.BlockSpec(memory_space=pl.ANY)
    sems = lambda *shape: [[pltpu.SemaphoreType.DMA(shape)] * 2]
    buffer = lambda *shape, kind=F32: pltpu.VMEM(shape, kind)
    most = GROUP
    arrays = (features, gain, bias, time_weight, time_bias, space_weight, space_bias)
    return pl.pallas_call(
        kernel,
        out_shape=jax.ShapeDtypeStruct((2 * frames, 4, 16, 256), F32),
        in_specs=[scalars, scalars] + [anywhere] * 7,
        out_specs=anywhere,
        scratch_shapes=[buffer(2, frames, 8, 512)] + [buffer(*array.shape) for array in arrays[1:]]
        + [buffer(3, 2, frames, 8, 512)]
        + [buffer(frames, 40, 512)] * 4
        + [buffer(frames, 24, 512), buffer(frames, 32, 512)]
        + [buffer(*shape, kind=jnp.int32) for shape in ((8, 128), (5, 8, 128), (4, 8, 128))]
        + [buffer(8, 128), buffer(16, 8, 128)] * 2
        + [buffer(2, *time_weight.shape, kind=BF16), buffer(2, 9, 512, 256, kind=BF16)]
        + [buffer(2, frames + 2, 32, 512, kind=BF16), buffer(most * 32, 1024), buffer(9, 2, most * 32, 512, kind=BF16)]
        + [buffer(2, most * 2, 4, 16, 128), buffer(2 * frames, 4, 16, 256)]
        + sems(3, 2, frames // GROUP) + sems(5, frames // GROUP) * 3 + sems(5) + sems(16) * 2
        + [pltpu.SemaphoreType.DMA((len(arrays) + 1,)), pltpu.SemaphoreType.DMA((frames,))],
        compiler_params=pltpu.CompilerParams(
            collective_id=0, has_side_effects=True, vmem_limit_bytes=58 * 2**20
        ),
    )(offsets, lengths, *arrays)


def on_device(features, lengths, offsets, norm_gain, norm_bias, time_weight, time_bias, space_weight, space_bias):
    frames, channels = features.shape[2], features.shape[-1]
    row = lambda array: array.reshape(1, -1)
    result = decoded(
        offsets, lengths, features.reshape(frames, 16, channels), row(norm_gain), row(norm_bias),
        time_weight, row(time_bias), space_weight, row(space_bias),
    )
    return result[None, None]


def solution(mesh):
    in_specs = (P("grp", "tile", None, None, None, None), P(), P("tile"), P(), P(), P(), P(), P(), P())
    out_specs = P("grp", "tile", None, None, None, None)
    return jax.shard_map(on_device, mesh=mesh, in_specs=in_specs, out_specs=out_specs, check_vma=False)
```
